128 devices in a mesh: dp: 4 (over x), expert: 32 (over z, y, core).
Axes of the slice: x: 4, y: 4, z: 4, core: 2. Of those that a mesh axis runs over, the one named last changes fastest.
Arguments:
- tokens: bfloat16 [16384, 7168], P(('dp', 'expert')), may hold values from -6 to 6
- out_grad: bfloat16 [16384, 7168], P(('dp', 'expert')), may hold values from -3 to 3
- expert_ids: int32 [16384, 1], P(('dp', 'expert')), may hold values from 0 to 31; in each aligned block of 128 rows (0 to 127, 128 to 255, ...) at most 6 rows name the same one
- route_probs: float32 [16384, 1], P(('dp', 'expert')), may hold values from 0.2 to 1
- w_gate: bfloat16 [32, 7168, 1024], P('expert', None, 'dp'), may hold values from -0.0625 to 0.0625
- w_up: bfloat16 [32, 7168, 1024], P('expert', None, 'dp'), may hold values from -0.0625 to 0.0625
- w_down: bfloat16 [32, 1024, 7168], P('expert', 'dp'), may hold values from -0.1875 to 0.1875
Outputs:
- token_grad: bfloat16 [16384, 7168], P(('dp', 'expert'))
- gate_grad: bfloat16 [32, 7168, 1024], P('expert', None, 'dp')
- up_grad: bfloat16 [32, 7168, 1024], P('expert', None, 'dp')
The draws below stay inside these ranges and needn't reach their ends.
Inputs may be any that keep to these rules, and one draw needn't show every extreme that they name: `expert_ids`: in the rows of one device (aligned blocks of 128 rows) no expert is named more than 6 times, a bound that some block reaches.
All inputs are finite; a program needn't handle non-finite values.
Results may differ from the reference program's by a relative error of at most 0.0064.
Values may be sent and summed in bfloat16 or wider, within the bound.
A program may use at most 192 MiB of HBM per device.

```python
import math
import jax
import jax.numpy as jnp
import numpy as np
from jax import lax

D = 7168
FFW = 1024
TOK_DEV = 128
ROUTES = 1
EXPERTS = 32
CAP = 6
ROWS = 768
TOKENS = 16384
N_DP = 4


def level_of(stream_key, dims, split, low, high):
    def one(position, shards_of):
        heights = jax.random.uniform(jax.random.fold_in(jax.random.fold_in(stream_key, 6), position), (shards_of,), jnp.float32, low / len(split), high / len(split))
        return jnp.repeat(jnp.exp(heights), dims[position] // shards_of).reshape((-1,) + (1,) * (len(dims) - position - 1))

    level = one(*split[0])
    for cut in split[1:]:
        level = level * one(*cut)
    return level


def assign_block(rng, own, number, rows, amount, top, most, lean):
    sequence = jax.random.permutation(rng, amount)
    packed, ordinary = shares(amount, rows * top, most, lean, True), shares(amount, rows * top, most, lean, False)
    places = jnp.arange(amount)

    def named(tallies, turn):
        used = int((tallies > 0).sum())
        fixed = max(1, used // 4)
        moved = fixed + (places - fixed + turn * (used - fixed)) % max(1, amount - fixed)
        return jnp.zeros((amount,), jnp.int32).at[sequence[jnp.where(places < fixed, places, moved)]].set(jnp.asarray(tallies, jnp.int32))

    tallies = jnp.where(number % 4 == 0, named(packed, number // 4), named(ordinary, number - number // 4 - 1))
    mixed = jax.random.permutation(jax.random.fold_in(own, 3), amount)
    donor, receiver = mixed[0:amount // 2 * 2:2], mixed[1:amount // 2 * 2:2]
    slack = jnp.minimum(tallies[donor] - 1, most - tallies[receiver]) // 2
    slack = jnp.where((donor == sequence[0]) | (receiver == sequence[0]) | (tallies[receiver] == 0), 0, jnp.maximum(slack, 0))
    moved = jax.random.randint(jax.random.fold_in(own, 4), (amount // 2,), 0, 1 << 20) % (slack + 1)
    tallies = tallies.at[donor].add(-moved).at[receiver].add(moved)
    members = jnp.searchsorted(jnp.cumsum(tallies), jnp.arange(rows * top), side="right").astype(jnp.int32)
    grid = members.reshape(top, rows).T
    grid = grid[jax.random.permutation(jax.random.fold_in(own, 1), rows)]
    turn = jax.random.randint(jax.random.fold_in(own, 2), (rows, 1), 0, top)
    return jnp.take_along_axis(grid, (jnp.arange(top)[None, :] + turn) % top, axis=1)


def shares(amount, total, bound, lean, full):
    weights = [(1 << 20) // math.isqrt(standing ** lean) + 1 for standing in range(1, amount + 1)]
    largest = bound if full else min(bound, max(-(-total // amount), total * weights[0] // sum(weights)))
    least = 1 if total - largest >= amount - 1 else 0
    given, spare = [largest] + [least] * (amount - 1), total - largest - least * (amount - 1)
    while spare > 0:
        movable = [i for i in range(1, amount) if given[i] < largest] or [i for i in range(1, amount) if given[i] < bound]
        pool, budget = sum([weights[i] for i in movable]), spare
        for i in movable:
            extra = min(bound - given[i], max(1, budget * weights[i] // pool), spare)
            given[i] = given[i] + extra
            spare = spare - extra
    return np.array(given)


def centred(rng, extent, deviation, limit, pieces=(), kind=jnp.bfloat16):
    array = jax.random.normal(rng, extent, jnp.float32) * deviation
    if len(pieces) > 0:
        array = level_of(rng, extent, pieces, -0.22, 0.18) * array
    return jnp.clip(array, min=-limit, max=limit).astype(kind)


def setup_inputs(seed: int = 0) -> dict:
    arg_keys = jax.random.split(jax.random.key(seed), 8)
    tokens = centred(arg_keys[0], (TOKENS, D), 1.0, 6.0, ((0, 128),))
    out_grad = centred(arg_keys[1], (TOKENS, D), 0.5, 3.0, ((0, 128),))
    expert_ids_keys = jax.random.split(jax.random.fold_in(arg_keys[2], 1), TOKENS // TOK_DEV)
    expert_ids_turns = jax.random.permutation(jax.random.fold_in(arg_keys[2], 3), TOKENS // TOK_DEV)
    expert_ids = jax.vmap(lambda own, number: assign_block(jax.random.fold_in(arg_keys[2], 2), own, number, TOK_DEV, EXPERTS, ROUTES, CAP, 2))(expert_ids_keys, expert_ids_turns).reshape((TOKENS, ROUTES))
    route_probs = jnp.clip(0.2 + 0.8 * jax.random.uniform(arg_keys[3], (TOKENS, ROUTES), jnp.float32) ** level_of(arg_keys[3], (TOKENS, ROUTES), ((0, 128),), -0.2, 0.2), 0.2, 1.0)
    w_gate = centred(arg_keys[4], (EXPERTS, D, FFW), D ** -0.5, 0.0625, ((0, 32), (2, 4)))
    w_up = centred(arg_keys[5], (EXPERTS, D, FFW), D ** -0.5, 0.0625, ((0, 32), (2, 4)))
    w_down = centred(arg_keys[6], (EXPERTS, FFW, D), FFW ** -0.5, 0.1875, ((0, 32), (1, 4)))
    return {"tokens": tokens, "out_grad": out_grad, "expert_ids": expert_ids, "route_probs": route_probs, "w_gate": w_gate, "w_up": w_up, "w_down": w_down}


def hidden_grads(x_rows, y_rows, gate_w, up_w, down_w):
    gate_val = jnp.dot(x_rows, gate_w, preferred_element_type=jnp.float32)
    up_val = jnp.dot(x_rows, up_w, preferred_element_type=jnp.float32)
    hidden_grad = lax.dot_general(y_rows, down_w, (((1,), (1,)), ((), ())), preferred_element_type=jnp.float32)
    sigmoid_val = jax.nn.sigmoid(gate_val)
    grad_up = (hidden_grad * gate_val * sigmoid_val).astype(jnp.bfloat16)
    grad_gate = (hidden_grad * up_val * sigmoid_val * (1.0 + gate_val * (1.0 - sigmoid_val))).astype(jnp.bfloat16)
    return grad_gate, grad_up


def contract_rows(x_rows, grads):
    return lax.dot_general(x_rows, grads, (((0,), (0,)), ((), ())), preferred_element_type=jnp.float32)


def reference(tokens, out_grad, expert_ids, route_probs, w_gate, w_up, w_down):
    route_count = expert_ids.shape[1]
    flat_ids = expert_ids.reshape(-1).astype(jnp.int32)
    total_routes = flat_ids.shape[0]
    sort_order = jnp.argsort(flat_ids, stable=True).astype(jnp.int32)
    labels = jnp.arange(EXPERTS, dtype=jnp.int32)
    counts = jnp.sum((flat_ids[:, None] == labels[None, :]).astype(jnp.int32), axis=0).astype(jnp.int32)
    offsets = (jnp.cumsum(counts) - counts).astype(jnp.int32)
    tok_rep = jnp.repeat(tokens, route_count, axis=0)
    scaled = (jnp.repeat(out_grad, route_count, axis=0).astype(jnp.float32) * route_probs.reshape(-1)[:, None]).astype(jnp.bfloat16)
    padding = jnp.zeros((ROWS, D), jnp.bfloat16)
    sorted_x = jnp.concatenate((tok_rep[sort_order], padding), axis=0)
    sorted_y = jnp.concatenate((scaled[sort_order], padding), axis=0)
    quarter = FFW // N_DP

    def one_expert(inputs):
        row_start, row_count, gate_w, up_w, down_w = inputs
        live_rows = (jnp.arange(ROWS, dtype=jnp.int32) < row_count)[:, None]
        zero_val = jnp.zeros((), jnp.bfloat16)
        x_rows = jnp.where(live_rows, lax.dynamic_slice_in_dim(sorted_x, row_start, ROWS, 0), zero_val)
        y_rows = jnp.where(live_rows, lax.dynamic_slice_in_dim(sorted_y, row_start, ROWS, 0), zero_val)
        grad_gate, grad_up = hidden_grads(x_rows, y_rows, gate_w, up_w, down_w)
        gate_out = contract_rows(x_rows, grad_gate).astype(jnp.bfloat16)
        up_out = contract_rows(x_rows, grad_up).astype(jnp.bfloat16)
        total_rows = jnp.zeros((ROWS, D), jnp.float32)
        for quarter_idx in range(N_DP):
            low = quarter_idx * quarter
            high = low + quarter
            partial_value = lax.dot_general(grad_gate[:, low:high], gate_w[:, low:high], (((1,), (1,)), ((), ())), preferred_element_type=jnp.float32)
            partial_value = partial_value + lax.dot_general(grad_up[:, low:high], up_w[:, low:high], (((1,), (1,)), ((), ())), preferred_element_type=jnp.float32)
            rounded = lax.optimization_barrier(partial_value.astype(jnp.bfloat16))
            total_rows = total_rows + rounded.astype(jnp.float32)
        return gate_out, up_out, total_rows.astype(jnp.bfloat16)

    gate_grad, up_grad, rows_out = lax.map(one_expert, (offsets, counts, w_gate, w_up, w_down))
    sorted_ids = flat_ids[sort_order]
    within = jnp.arange(total_routes, dtype=jnp.int32) - offsets[sorted_ids]
    grad_sorted = rows_out[sorted_ids, within]
    grad_routes = jnp.zeros((total_routes, D), jnp.bfloat16).at[sort_order].set(grad_sorted)
    token_grad = jnp.sum(grad_routes.reshape(-1, route_count, D).astype(jnp.float32), axis=1).astype(jnp.bfloat16)
    return token_grad, gate_grad, up_grad
```

```python
import jax
import jax.numpy as jnp
from jax import lax
from jax.experimental import pallas as pl
from jax.experimental.pallas import tpu as pltpu
from jax.sharding import PartitionSpec as P

MESH = pl.DeviceIdType.MESH
F32, BF16 = jnp.float32, jnp.bfloat16
CHUNKS = 3
PER = 2
OCT = 8
SLAB = PER * OCT
X, Y = 0, 1
NN = (((1,), (0,)), ((), ()))
NT = (((1,), (1,)), ((), ()))
TN = (((0,), (0,)), ((), ()))


def dot(a, b, dims=NN):
    return lax.dot_general(a, b, dims, preferred_element_type=F32)


def iota(shape, axis):
    return lax.broadcasted_iota(jnp.int32, shape, axis)


def kernel(
    ids_col, ids_row, probs, tok_hbm, og_hbm, wg_hbm, wu_hbm, wd_hbm,
    tg_hbm, gg_hbm, ug_hbm,
    tok, q, wg, wu, wd, send, recv, rows, relay, fin, back, acc, grads, stage,
    load_sem, disp_send, disp_recv, own_sem, ag_send, ag_recv, rs_send, rs_recv,
    ret_send, ret_recv, retown_sem, out_sem,
):
    n_x = lax.axis_size("dp")
    n_e = lax.axis_size("expert")
    me_x = lax.axis_index("dp")
    me_e = lax.axis_index("expert")
    nbr = (lax.rem(me_x + 1, n_x), lax.rem(me_x + n_x - 1, n_x))
    far = lax.rem(me_x + 2, n_x)
    toks, width = tok_hbm.shape
    oct_w = width // OCT
    quarter = wg_hbm.shape[1]
    half = n_e
    gs = n_e // 2
    chunk_rows = n_x * n_e * PER
    log_half = half.bit_length() - 1

    loads = []
    for a, src in ((X, tok_hbm), (Y, og_hbm)):
        for j in range(OCT):
            loads.append(
                pltpu.make_async_copy(
                    src.at[:, pl.ds(j * oct_w, oct_w)], tok.at[a, j], load_sem.at[a, j]
                )
            )
            loads[-1].start()
    weights = [
        pltpu.make_async_copy(src, dst, load_sem.at[2, i])
        for i, (src, dst) in enumerate(((wg_hbm, wg), (wu_hbm, wu), (wd_hbm, wd)))
    ]
    for w in weights:
        w.start()

    barrier = pltpu.get_barrier_semaphore()

    def greet(d, carry):
        pl.semaphore_signal(
            barrier, inc=1, device_id=(me_x, lax.rem(me_e + d, n_e)), device_id_type=MESH
        )
        return carry

    lax.fori_loop(1, n_e, greet, 0)
    for x in nbr:
        pl.semaphore_signal(barrier, inc=1, device_id=(x, me_e), device_id_type=MESH)

    same = ids_col[...] == ids_row[...]
    first, second = iota((toks, toks), 0), iota((toks, toks), 1)
    rank_row = jnp.sum(jnp.where(same & (first < second), 1, 0), axis=0, keepdims=True)
    rank_col = jnp.sum(jnp.where(same & (second < first), 1, 0), axis=1, keepdims=True)
    key_row = ids_row[...] * PER + (rank_row & 1)
    key_col = ids_col[...] * PER + (rank_col & 1)

    n_slab_rows = n_e * SLAB
    step = min(128, n_slab_rows)

    def build_q(c):
        keyc = jnp.where((rank_row >> 1) == c, key_row, -1)
        i = iota((n_slab_rows, 1), 0)
        for j in range(OCT):
            want = jnp.where(((i >> 1) & (OCT - 1)) == j, (i >> 4) * PER + (i & 1), -2)
            q[:, j * toks : (j + 1) * toks] = jnp.where(want == keyc, 1.0, 0.0).astype(BF16)

    def fill(a, c):
        def body(m, carry):
            part = q[pl.ds(pl.multiple_of(m * step, step), step), :]
            out = dot(part, tok[a].reshape(OCT * toks, oct_w)).astype(BF16)
            send[a, c, pl.ds(m * (step // SLAB), step // SLAB)] = out.reshape(
                step // SLAB, SLAB, oct_w
            )
            return carry

        lax.fori_loop(0, n_slab_rows // step, body, 0)

    def scatter(src, dst, send_sem, recv_sem, self_sem):
        pltpu.make_async_copy(src.at[me_e], dst.at[me_e], self_sem).start()

        def body(d, carry):
            peer = lax.rem(me_e + d, n_e)
            pltpu.make_async_remote_copy(
                src_ref=src.at[peer],
                dst_ref=dst.at[me_e],
                send_sem=send_sem,
                recv_sem=recv_sem,
                device_id=(me_x, peer),
                device_id_type=MESH,
            ).start()
            return carry

        lax.fori_loop(1, n_e, body, 0)

    def scattered(src, dst, send_sem, recv_sem):
        return pltpu.make_async_remote_copy(
            src_ref=src.at[pl.ds(0, n_e - 1)],
            dst_ref=dst.at[pl.ds(0, n_e - 1)],
            send_sem=send_sem,
            recv_sem=recv_sem,
            device_id=(nbr[0], me_e),
            device_id_type=MESH,
        )

    def dispatch(a, c):
        scatter(
            send.at[a, c], recv.at[a, c], disp_send.at[a, c], disp_recv.at[a, c], own_sem.at[a, c]
        )

    def dispatched(a, c):
        return scattered(send.at[a, c], recv.at[a, c], disp_send.at[a, c], disp_recv.at[a, c])

    def hop(a, c, block, h, way, slot):
        ref = rows.at[a, c, block * 2 + h]
        return pltpu.make_async_remote_copy(
            src_ref=ref,
            dst_ref=ref,
            send_sem=ag_send.at[a, c, way, slot],
            recv_sem=ag_recv.at[a, c, way, slot],
            device_id=(nbr[way], me_e),
            device_id_type=MESH,
        )

    size = gs * SLAB

    def perm(row, col):
        j, rest = row >> log_half, row & (half - 1)
        return jnp.where(col == (rest >> 1) * SLAB + j * PER + (rest & 1), 1.0, 0.0).astype(BF16)

    def own(a, c):
        pltpu.make_async_copy(send.at[a, c, me_e], recv.at[a, c, me_e], own_sem.at[a, c]).wait()
        dispatched(a, c).wait_recv()
        order = perm(iota((size, size), 0), iota((size, size), 1))
        for h in range(2):
            block = recv[a, c, h * gs : (h + 1) * gs].reshape(size, oct_w)
            out = dot(order, block).astype(BF16)
            for j in range(OCT):
                rows[a, c, me_x * 2 + h, :, j * oct_w : (j + 1) * oct_w] = out[
                    j * half : (j + 1) * half
                ]
        hop(a, c, me_x, 0, 0, 0).start()
        hop(a, c, me_x, 1, 1, 1).start()
        hop(a, c, me_x, 1, 0, 1).start()
        hop(a, c, me_x, 0, 1, 0).start()

    def arrive(a, c):
        for way in range(2):
            block = nbr[1 - way]
            hop(a, c, block, way, way, way).wait_recv()
            hop(a, c, block, way, way, 2).start()

    def complete(a, c):
        for way in range(2):
            hop(a, c, nbr[1 - way], 1 - way, way, 1 - way).wait_recv()
            hop(a, c, far, way, way, 2).wait_recv()

    def sent(a, c):
        for way in range(2):
            for slot in range(2):
                hop(a, c, me_x, slot, way, slot).wait_send()
            hop(a, c, nbr[1 - way], way, way, 2).wait_send()

    kw = width // 4

    def forward(c):
        def body(k, carry):
            cols = pl.ds(pl.multiple_of(k * kw, 128), kw)
            x = rows[X, c, :, :, cols].reshape(chunk_rows, kw)
            g = dot(x, wg[cols, :])
            u = dot(x, wu[cols, :])

            @pl.when(k == 0)
            def _():
                acc[0] = g
                acc[1] = u

            @pl.when(k > 0)
            def _():
                acc[0] += g
                acc[1] += u

            return carry

        lax.fori_loop(0, 4, body, 0)

    bw = 512 if width % 512 == 0 else 128

    def backward(c):
        def body(k, carry):
            cols = pl.ds(pl.multiple_of(k * kw, 128), kw)
            y = rows[Y, c, :, :, cols].reshape(chunk_rows, kw)
            h = dot(y, wd[:, cols], NT)

            @pl.when(k == 0)
            def _():
                acc[2] = h

            @pl.when(k > 0)
            def _():
                acc[2] += h

            return carry

        lax.fori_loop(0, 4, body, 0)
        gate_val, up_val, hidden = acc[0], acc[1], acc[2]
        s = jax.nn.sigmoid(gate_val)
        grad_up = (hidden * gate_val * s).astype(BF16)
        grad_gate = (hidden * up_val * s * (1.0 + gate_val * (1.0 - s))).astype(BF16)
        grads[c * chunk_rows : (c + 1) * chunk_rows, :quarter] = grad_gate
        grads[c * chunk_rows : (c + 1) * chunk_rows, quarter:] = grad_up

        def part(d, carry):
            cols = pl.ds(pl.multiple_of(d * bw, 128), bw)
            g = grads[c * chunk_rows : (c + 1) * chunk_rows, :quarter]
            u = grads[c * chunk_rows : (c + 1) * chunk_rows, quarter:]
            out = dot(g, wg[cols, :], NT) + dot(u, wu[cols, :], NT)
            rows[Y, c, :, :, cols] = out.astype(BF16).reshape(2 * n_x, half, bw)
            return carry

        lax.fori_loop(0, width // bw, part, 0)

    def back_of(c):
        return (recv.at[X, 0], recv.at[Y, 0], back)[c]

    def toward(c, way, slot):
        dst_block = far if slot == 0 else nbr[way]
        h = (way, 1 - way, way)[slot]
        src = rows.at[Y, c, dst_block * 2 + h]
        dst = relay.at[c, way] if slot == 0 else fin.at[c, way, h]
        return pltpu.make_async_remote_copy(
            src_ref=src,
            dst_ref=dst,
            send_sem=rs_send.at[c, way, slot],
            recv_sem=rs_recv.at[c, way, slot],
            device_id=(nbr[way], me_e),
            device_id_type=MESH,
        )

    def start_reduce(c):
        for slot in range(2):
            for way in range(2):
                toward(c, way, slot).start()

    def pass_on(c):
        for way in range(2):
            toward(c, way, 0).wait_recv()

            def body(d, carry):
                cols = pl.ds(pl.multiple_of(d * bw, 128), bw)
                at = nbr[way] * 2 + way
                total = rows[Y, c, at, :, cols].astype(F32) + relay[c, way, :, cols].astype(F32)
                rows[Y, c, at, :, cols] = total.astype(BF16)
                return carry

            lax.fori_loop(0, width // bw, body, 0)
            toward(c, way, 2).start()

    def finish(c):
        dispatched(X, c).wait_send()
        order = perm(iota((size, size), 1), iota((size, size), 0))
        for way in range(2):
            for slot in (1, 2):
                toward(c, way, slot).wait_recv()
        for h in range(2):
            blocks = []
            for j in range(OCT):
                cols = slice(j * oct_w, (j + 1) * oct_w)
                total = (
                    rows[Y, c, me_x * 2 + h, :, cols].astype(F32)
                    + fin[c, 0, h, :, cols].astype(F32)
                    + fin[c, 1, h, :, cols].astype(F32)
                )
                blocks.append(total.astype(BF16))
            out = dot(order, jnp.concatenate(blocks, axis=0)).astype(BF16)
            send[X, c, h * gs : (h + 1) * gs] = out.reshape(gs, SLAB, oct_w)
        scatter(send.at[X, c], back_of(c), ret_send.at[c], ret_recv.at[c], retown_sem.at[c])

    def weight_grads():
        def tile(i, slot):
            cols = pl.ds(pl.multiple_of(i * bw, 128), bw)
            return [
                pltpu.make_async_copy(stage.at[slot, o], dst.at[cols, :], out_sem.at[slot, o])
                for o, dst in ((0, gg_hbm), (1, ug_hbm))
            ]

        def body(i, carry):
            slot = lax.rem(i, 2)

            @pl.when(i >= 2)
            def _():
                for copy in tile(i - 2, slot):
                    copy.wait()

            cols = pl.ds(pl.multiple_of(i * bw, 128), bw)
            x = rows[X, :, :, :, cols].reshape(CHUNKS * chunk_rows, bw)
            out = dot(x, grads[...], TN).astype(BF16)
            stage[slot, 0] = out[:, :quarter]
            stage[slot, 1] = out[:, quarter:]
            for copy in tile(i, slot):
                copy.start()
            return carry

        n = width // bw
        lax.fori_loop(0, n, body, 0)
        for i in (n - 2, n - 1):
            for copy in tile(i, i % 2):
                copy.wait()

    def token_grads():
        for c in range(CHUNKS):
            pltpu.make_async_copy(send.at[X, c, me_e], back_of(c).at[me_e], retown_sem.at[c]).wait()
            scattered(send.at[X, c], back_of(c), ret_send.at[c], ret_recv.at[c]).wait_recv()
        i = iota((1, n_slab_rows), 1)

        def body(j, carry):
            want = jnp.where(((i >> 1) & (OCT - 1)) == j, (i >> 4) * PER + (i & 1), -2)
            total = None
            for c in range(CHUNKS):
                keyc = jnp.where((rank_col >> 1) == c, key_col, -1)
                place = jnp.where(keyc == want, 1.0, 0.0).astype(BF16)
                one = dot(place, back_of(c)[...].reshape(n_slab_rows, oct_w))
                total = one if total is None else total + one
            tok[X, j] = total.astype(BF16)
            return carry

        lax.fori_loop(0, OCT, body, 0)
        copies = [
            pltpu.make_async_copy(
                tok.at[X, j], tg_hbm.at[:, pl.ds(j * oct_w, oct_w)], load_sem.at[0, j]
            )
            for j in range(OCT)
        ]
        for copy in copies:
            copy.start()
        for copy in copies:
            copy.wait()

    build_q(0)
    for copy in loads[:OCT]:
        copy.wait()
    fill(X, 0)
    pl.semaphore_wait(barrier, n_e - 1 + 2)
    dispatch(X, 0)
    for copy in loads[OCT:]:
        copy.wait()
    for j in range(OCT):
        tok[Y, j] = (tok[Y, j].astype(F32) * probs[...]).astype(BF16)
    fill(Y, 0)
    dispatch(Y, 0)
    build_q(1)
    fill(X, 1)
    dispatch(X, 1)
    own(X, 0)
    fill(Y, 1)
    dispatch(Y, 1)
    own(Y, 0)
    build_q(2)
    for a in (X, Y):
        fill(a, 2)
        dispatch(a, 2)
    arrive(X, 0)
    for copy in weights:
        copy.wait()
    own(X, 1)
    arrive(Y, 0)
    complete(X, 0)
    forward(0)
    own(Y, 1)
    arrive(X, 1)
    complete(Y, 0)
    sent(Y, 0)
    backward(0)
    start_reduce(0)
    own(X, 2)
    arrive(Y, 1)
    pass_on(0)
    complete(X, 1)
    forward(1)
    own(Y, 2)
    arrive(X, 2)
    complete(Y, 1)
    sent(Y, 1)
    backward(1)
    start_reduce(1)
    finish(0)
    arrive(Y, 2)
    pass_on(1)
    complete(X, 2)
    forward(2)
    complete(Y, 2)
    sent(Y, 2)
    backward(2)
    start_reduce(2)
    finish(1)
    pass_on(2)
    weight_grads()
    finish(2)
    token_grads()
    for c in range(CHUNKS):
        sent(X, c)
        dispatched(Y, c).wait_send()
        for way in range(2):
            for slot in range(3):
                toward(c, way, slot).wait_send()
        scattered(send.at[X, c], back_of(c), ret_send.at[c], ret_recv.at[c]).wait_send()


def local(tokens, out_grad, expert_ids, route_probs, w_gate, w_up, w_down):
    n_e = lax.axis_size("expert")
    n_x = lax.axis_size("dp")
    toks, width = tokens.shape
    gate_w, up_w, down_w = w_gate[0], w_up[0], w_down[0]
    quarter = gate_w.shape[1]
    oct_w = width // OCT
    chunk_rows = n_x * n_e * PER
    bw = 512 if width % 512 == 0 else 128
    vmem = pl.BlockSpec(memory_space=pltpu.VMEM)
    hbm = pl.BlockSpec(memory_space=pl.ANY)
    dma = pltpu.SemaphoreType.DMA
    token_grad, gate_grad, up_grad = pl.pallas_call(
        kernel,
        out_shape=(
            jax.ShapeDtypeStruct((toks, width), BF16),
            jax.ShapeDtypeStruct((width, quarter), BF16),
            jax.ShapeDtypeStruct((width, quarter), BF16),
        ),
        in_specs=[vmem] * 3 + [hbm] * 5,
        out_specs=(hbm, hbm, hbm),
        scratch_shapes=[
            pltpu.VMEM((2, OCT, toks, oct_w), BF16),
            pltpu.VMEM((n_e * SLAB, OCT * toks), BF16),
            pltpu.VMEM((width, quarter), BF16),
            pltpu.VMEM((width, quarter), BF16),
            pltpu.VMEM((quarter, width), BF16),
            pltpu.VMEM((2, CHUNKS, n_e, SLAB, oct_w), BF16),
            pltpu.VMEM((2, CHUNKS, n_e, SLAB, oct_w), BF16),
            pltpu.VMEM((2, CHUNKS, 2 * n_x, n_e, width), BF16),
            pltpu.VMEM((CHUNKS, 2, n_e, width), BF16),
            pltpu.VMEM((CHUNKS, 2, 2, n_e, width), BF16),
            pltpu.VMEM((n_e, SLAB, oct_w), BF16),
            pltpu.VMEM((3, chunk_rows, quarter), F32),
            pltpu.VMEM((CHUNKS * chunk_rows, 2 * quarter), BF16),
            pltpu.VMEM((2, 2, bw, quarter), BF16),
            dma((3, OCT)),
            dma((2, CHUNKS)),
            dma((2, CHUNKS)),
            dma((2, CHUNKS)),
            dma((2, CHUNKS, 2, 3)),
            dma((2, CHUNKS, 2, 3)),
            dma((CHUNKS, 2, 3)),
            dma((CHUNKS, 2, 3)),
            dma((CHUNKS,)),
            dma((CHUNKS,)),
            dma((CHUNKS,)),
            dma((2, 2)),
        ],
        compiler_params=pltpu.CompilerParams(
            collective_id=0, has_side_effects=True, vmem_limit_bytes=127 * 2**19
        ),
    )(
        expert_ids,
        expert_ids.reshape(1, toks),
        route_probs,
        tokens,
        out_grad,
        gate_w,
        up_w,
        down_w,
    )
    return token_grad, gate_grad[None], up_grad[None]


def solution(mesh):
    in_specs = (
        P(("dp", "expert"), None),
        P(("dp", "expert"), None),
        P(("dp", "expert"), None),
        P(("dp", "expert"), None),
        P("expert", None, "dp"),
        P("expert", None, "dp"),
        P("expert", "dp", None),
    )
    out_specs = (P(("dp", "expert"), None), P("expert", None, "dp"), P("expert", None, "dp"))
    return jax.shard_map(local, mesh=mesh, in_specs=in_specs, out_specs=out_specs, check_vma=False)
```

```python
import jax
import jax.numpy as jnp
from jax import lax
from jax.experimental import pallas as pl
from jax.experimental.pallas import tpu as pltpu
from jax.sharding import PartitionSpec as P

MESH = pl.DeviceIdType.MESH
F32, BF16 = jnp.float32, jnp.bfloat16
CHUNKS = 3
PER = 2
OCT = 8
SLAB = PER * OCT
X, Y = 0, 1
NN = (((1,), (0,)), ((), ()))
NT = (((1,), (1,)), ((), ()))
TN = (((0,), (0,)), ((), ()))


def dot(a, b, dims=NN):
    return lax.dot_general(a, b, dims, preferred_element_type=F32)


def iota(shape, axis):
    return lax.broadcasted_iota(jnp.int32, shape, axis)


def kernel(
    ids_ref, probs_ref, tok_hbm, og_hbm, wg_hbm, wu_hbm, wd_hbm,
    tg_hbm, gg_hbm, ug_hbm, fin_hbm,
    tok, q, wg, wu, wd, wp, send, recv, rows, relay, fin, back, acc, part_acc, ex_out, ex_in, grads,
    load_sem, disp_send, disp_recv, own_sem, ag_send, ag_recv, y_send, y_recv, w_send, w_recv,
    ex_send, ex_recv, rs_send, rs_recv, ret_send, ret_recv, retown_sem, out_sem, fin_sem,
):
    n_x = lax.axis_size("dp")
    n_e = lax.axis_size("expert")
    me_x = lax.axis_index("dp")
    me_e = lax.axis_index("expert")
    nbr = (lax.rem(me_x + 1, n_x), lax.rem(me_x + n_x - 1, n_x))
    far = lax.rem(me_x + 2, n_x)
    pair = (me_x + 1 - 2 * lax.rem(me_x, 2), n_x - 1 - me_x)
    toks, width = tok_hbm.shape
    oct_w = width // OCT
    quarter = wg_hbm.shape[1]
    half = n_e
    gs = n_e // 2
    chunk_rows = n_x * n_e * PER
    log_half = half.bit_length() - 1

    loads = []
    for a, src in ((X, tok_hbm), (Y, og_hbm)):
        for j in range(OCT):
            loads.append(
                pltpu.make_async_copy(
                    src.at[:, pl.ds(j * oct_w, oct_w)], tok.at[a, j], load_sem.at[a, j]
                )
            )
            loads[-1].start()
    weights = [
        pltpu.make_async_copy(src, dst, load_sem.at[2, i])
        for i, (src, dst) in enumerate(((wg_hbm, wg), (wu_hbm, wu), (wd_hbm, wd)))
    ]
    for w in weights:
        w.start()

    barrier = pltpu.get_barrier_semaphore()

    def greet(d, carry):
        pl.semaphore_signal(
            barrier, inc=1, device_id=(me_x, lax.rem(me_e + d, n_e)), device_id_type=MESH
        )
        return carry

    lax.fori_loop(1, n_e, greet, 0)
    for x in nbr:
        pl.semaphore_signal(barrier, inc=1, device_id=(x, me_e), device_id_type=MESH)

    first, second = iota((toks, toks), 0), iota((toks, toks), 1)

    def upright(row):
        return jnp.sum(jnp.where(first == second, row, jnp.zeros_like(row)), axis=1, keepdims=True)

    ids_row = ids_ref[...]
    ids_col, probs = upright(ids_row), upright(probs_ref[...])
    same = ids_col == ids_row
    rank_row = jnp.sum(jnp.where(same & (first < second), 1, 0), axis=0, keepdims=True)
    rank_col = jnp.sum(jnp.where(same & (second < first), 1, 0), axis=1, keepdims=True)
    key_row = ids_row * PER + (rank_row & 1)
    key_col = ids_col * PER + (rank_col & 1)

    n_slab_rows = n_e * SLAB
    step = min(128, n_slab_rows)

    def build_q(c):
        keyc = jnp.where((rank_row >> 1) == c, key_row, -1)
        i = iota((n_slab_rows, 1), 0)
        for j in range(OCT):
            want = jnp.where(((i >> 1) & (OCT - 1)) == j, (i >> 4) * PER + (i & 1), -2)
            q[:n_slab_rows, j * toks : (j + 1) * toks] = jnp.where(want == keyc, 1.0, 0.0).astype(BF16)

    def fill(a, c):
        def body(m, carry):
            part = q[pl.ds(pl.multiple_of(m * step, step), step), : OCT * toks]
            out = dot(part, tok[a].reshape(OCT * toks, oct_w)).astype(BF16)
            send[a, c, pl.ds(m * (step // SLAB), step // SLAB)] = out.reshape(
                step // SLAB, SLAB, oct_w
            )
            return carry

        lax.fori_loop(0, n_slab_rows // step, body, 0)

    def scatter(src, dst, send_sem, recv_sem, self_sem):
        pltpu.make_async_copy(src.at[me_e], dst.at[me_e], self_sem).start()

        def body(d, carry):
            peer = lax.rem(me_e + d, n_e)
            pltpu.make_async_remote_copy(
                src_ref=src.at[peer],
                dst_ref=dst.at[me_e],
                send_sem=send_sem,
                recv_sem=recv_sem,
                device_id=(me_x, peer),
                device_id_type=MESH,
            ).start()
            return carry

        lax.fori_loop(1, n_e, body, 0)

    def scattered(src, dst, send_sem, recv_sem):
        return pltpu.make_async_remote_copy(
            src_ref=src.at[pl.ds(0, n_e - 1)],
            dst_ref=dst.at[pl.ds(0, n_e - 1)],
            send_sem=send_sem,
            recv_sem=recv_sem,
            device_id=(nbr[0], me_e),
            device_id_type=MESH,
        )

    def dispatch(a, c):
        scatter(
            send.at[a, c], recv.at[a, c], disp_send.at[a, c], disp_recv.at[a, c], own_sem.at[a, c]
        )

    def dispatched(a, c):
        return scattered(send.at[a, c], recv.at[a, c], disp_send.at[a, c], disp_recv.at[a, c])

    def hop(a, c, block, h, way, slot):
        ref = rows.at[a, c, block * 2 + h]
        return pltpu.make_async_remote_copy(
            src_ref=ref,
            dst_ref=ref,
            send_sem=ag_send.at[c, way, slot],
            recv_sem=ag_recv.at[c, way, slot],
            device_id=(nbr[way], me_e),
            device_id_type=MESH,
        )

    size = gs * SLAB

    def perm(row, col):
        j, rest = row >> log_half, row & (half - 1)
        return jnp.where(col == (rest >> 1) * SLAB + j * PER + (rest & 1), 1.0, 0.0).astype(BF16)

    def collect(a, c):
        pltpu.make_async_copy(send.at[a, c, me_e], recv.at[a, c, me_e], own_sem.at[a, c]).wait()
        dispatched(a, c).wait_recv()
        order = perm(iota((size, size), 0), iota((size, size), 1))
        for h in range(2):
            block = recv[a, c, h * gs : (h + 1) * gs].reshape(size, oct_w)
            out = dot(order, block).astype(BF16)
            for j in range(OCT):
                rows[a, c, me_x * 2 + h, :, j * oct_w : (j + 1) * oct_w] = out[
                    j * half : (j + 1) * half
                ]

    def own(c):
        collect(X, c)
        hop(X, c, me_x, 0, 0, 0).start()
        hop(X, c, me_x, 1, 1, 1).start()
        hop(X, c, me_x, 1, 0, 1).start()
        hop(X, c, me_x, 0, 1, 0).start()

    wide = width // 2

    def swap_weight(i):
        return pltpu.make_async_remote_copy(
            src_ref=wd_hbm.at[:, pl.ds(i * wide, wide)],
            dst_ref=wp.at[i],
            send_sem=w_send.at[i],
            recv_sem=w_recv.at[i],
            device_id=(pair[i], me_e),
            device_id_type=MESH,
        )

    def lend(c, i, block):
        ref = rows.at[Y, c, pl.ds(block * 2, 2), :, pl.ds(i * wide, wide)]
        return pltpu.make_async_remote_copy(
            src_ref=ref,
            dst_ref=ref,
            send_sem=y_send.at[c, i],
            recv_sem=y_recv.at[c, i],
            device_id=(pair[1 - i], me_e),
            device_id_type=MESH,
        )

    def own_y(c):
        collect(Y, c)
        for i in range(2):
            lend(c, i, me_x).start()

    def exchange(c, i):
        return pltpu.make_async_remote_copy(
            src_ref=ex_out.at[c, i],
            dst_ref=ex_in.at[c, i],
            send_sem=ex_send.at[c, i],
            recv_sem=ex_recv.at[c, i],
            device_id=(pair[i], me_e),
            device_id_type=MESH,
        )

    def arrive(c):
        for way in range(2):
            block = nbr[1 - way]
            hop(X, c, block, way, way, way).wait_recv()
            hop(X, c, block, way, way, 2).start()

    def complete(c):
        for way in range(2):
            hop(X, c, nbr[1 - way], 1 - way, way, 1 - way).wait_recv()
            hop(X, c, far, way, way, 2).wait_recv()

    def sent(c):
        for way in range(2):
            for slot in range(2):
                hop(X, c, me_x, slot, way, slot).wait_send()
            hop(X, c, nbr[1 - way], way, way, 2).wait_send()

    kw = width // 4

    def forward(c):
        def body(k, carry):
            cols = pl.ds(pl.multiple_of(k * kw, 128), kw)
            x = rows[X, c, :, :, cols].reshape(chunk_rows, kw)
            g = dot(x, wg[cols, :]).reshape(acc.shape[1:])
            u = dot(x, wu[cols, :]).reshape(acc.shape[1:])

            @pl.when(k == 0)
            def _():
                acc[0] = g
                acc[1] = u

            @pl.when(k > 0)
            def _():
                acc[0] += g
                acc[1] += u

            return carry

        lax.fori_loop(0, 4, body, 0)

    bw = 512 if width % 512 == 0 else 128

    block_rows = 2 * half

    def partial(c):
        for i in range(2):
            lend(c, i, pair[1 - i]).wait_recv()
            if c == 0:
                swap_weight(i).wait_recv()

            def body(k, carry):
                step_w = wide // 4
                near = pl.ds(pl.multiple_of(k * step_w, 128), step_w)
                cols = pl.ds(pl.multiple_of(i * wide + k * step_w, 128), step_w)
                y = jnp.concatenate(
                    [
                        rows[Y, c, pl.ds(p * 2, 2), :, cols].reshape(block_rows, step_w)
                        for p in (me_x, pair[1 - i])
                    ],
                    axis=0,
                )
                mine = dot(y, wd[:, cols], NT)
                lent = dot(y, wp[i, :, near], NT)

                @pl.when(k == 0)
                def _():
                    part_acc[0] = mine
                    part_acc[1] = lent

                @pl.when(k > 0)
                def _():
                    part_acc[0] += mine
                    part_acc[1] += lent

                return carry

            lax.fori_loop(0, 4, body, 0)
            ex_out[c, i] = part_acc[1].astype(BF16)
            exchange(c, i).start()
            if i == 0:
                acc[2, me_x] = part_acc[0, :block_rows]
            else:
                acc[2, me_x] += part_acc[0, :block_rows]
            acc[2, pair[1 - i]] = part_acc[0, block_rows:]

    def backward(c):
        for i in range(2):
            exchange(c, i).wait_recv()
            lend(c, i, me_x).wait_send()
        for i in range(2):
            acc[2, pair[i]] += ex_in[c, i, :block_rows].astype(F32)
        acc[2, far] = ex_in[c, 0, block_rows:].astype(F32) + ex_in[c, 1, block_rows:].astype(F32)
        gate_val, up_val, hidden = (acc[n].reshape(chunk_rows, quarter) for n in range(3))
        s = jax.nn.sigmoid(gate_val)
        grad_up = (hidden * gate_val * s).astype(BF16)
        grad_gate = (hidden * up_val * s * (1.0 + gate_val * (1.0 - s))).astype(BF16)
        grads[c * chunk_rows : (c + 1) * chunk_rows, :quarter] = grad_gate
        grads[c * chunk_rows : (c + 1) * chunk_rows, quarter:] = grad_up

        def part(d, carry):
            cols = pl.ds(pl.multiple_of(d * bw, 128), bw)
            g = grads[c * chunk_rows : (c + 1) * chunk_rows, :quarter]
            u = grads[c * chunk_rows : (c + 1) * chunk_rows, quarter:]
            out = dot(g, wg[cols, :], NT) + dot(u, wu[cols, :], NT)
            rows[Y, c, :, :, cols] = out.astype(BF16).reshape(2 * n_x, half, bw)
            return carry

        lax.fori_loop(0, width // bw, part, 0)

    def back_of(c):
        return (recv.at[X, 0], recv.at[Y, 0], back)[c]

    def last_of(c):
        return fin if c == CHUNKS - 1 else fin_hbm.at[c]

    def toward(c, way, slot):
        dst_block = far if slot == 0 else nbr[way]
        h = (way, 1 - way, way)[slot]
        src = rows.at[Y, c, dst_block * 2 + h]
        dst = relay.at[c, way] if slot == 0 else last_of(c).at[way, h]
        return pltpu.make_async_remote_copy(
            src_ref=src,
            dst_ref=dst,
            send_sem=rs_send.at[c, way, slot],
            recv_sem=rs_recv.at[c, way, slot],
            device_id=(nbr[way], me_e),
            device_id_type=MESH,
        )

    def start_reduce(c):
        for slot in range(2):
            for way in range(2):
                toward(c, way, slot).start()

    def pass_on(c):
        for way in range(2):
            toward(c, way, 0).wait_recv()

            def body(d, carry):
                cols = pl.ds(pl.multiple_of(d * bw, 128), bw)
                at = nbr[way] * 2 + way
                total = rows[Y, c, at, :, cols].astype(F32) + relay[c, way, :, cols].astype(F32)
                rows[Y, c, at, :, cols] = total.astype(BF16)
                return carry

            lax.fori_loop(0, width // bw, body, 0)
            toward(c, way, 2).start()

    def finish(c):
        dispatched(X, c).wait_send()
        order = perm(iota((size, size), 1), iota((size, size), 0))
        for way in range(2):
            for slot in (1, 2):
                toward(c, way, slot).wait_recv()
        for h in range(2):
            if c < CHUNKS - 1:
                fetch = [
                    pltpu.make_async_copy(fin_hbm.at[c, way, h], relay.at[c, way], fin_sem.at[way])
                    for way in range(2)
                ]
                for copy in fetch:
                    copy.start()
                for copy in fetch:
                    copy.wait()
            came = (relay.at[c, 0], relay.at[c, 1]) if c < CHUNKS - 1 else (fin.at[0, h], fin.at[1, h])
            blocks = []
            for j in range(OCT):
                cols = slice(j * oct_w, (j + 1) * oct_w)
                total = (
                    rows[Y, c, me_x * 2 + h, :, cols].astype(F32)
                    + came[0][:, cols].astype(F32)
                    + came[1][:, cols].astype(F32)
                )
                blocks.append(total.astype(BF16))
            out = dot(order, jnp.concatenate(blocks, axis=0)).astype(BF16)
            send[X, c, h * gs : (h + 1) * gs] = out.reshape(gs, SLAB, oct_w)
        scatter(send.at[X, c], back_of(c), ret_send.at[c], ret_recv.at[c], retown_sem.at[c])

    def stage(slot, o):
        return q.at[pl.ds(0, bw), pl.ds(pl.multiple_of((slot * 2 + o) * quarter, 128), quarter)]

    def weight_grads():
        def tile(i, slot):
            cols = pl.ds(pl.multiple_of(i * bw, 128), bw)
            return [
                pltpu.make_async_copy(stage(slot, o), dst.at[cols, :], out_sem.at[slot, o])
                for o, dst in ((0, gg_hbm), (1, ug_hbm))
            ]

        def body(i, carry):
            slot = lax.rem(i, 2)

            @pl.when(i >= 2)
            def _():
                for copy in tile(i - 2, slot):
                    copy.wait()

            cols = pl.ds(pl.multiple_of(i * bw, 128), bw)
            x = rows[X, :, :, :, cols].reshape(CHUNKS * chunk_rows, bw)
            out = dot(x, grads[...], TN).astype(BF16)
            stage(slot, 0)[...] = out[:, :quarter]
            stage(slot, 1)[...] = out[:, quarter:]
            for copy in tile(i, slot):
                copy.start()
            return carry

        n = width // bw
        lax.fori_loop(0, n, body, 0)
        for i in (n - 2, n - 1):
            for copy in tile(i, i % 2):
                copy.wait()

    def token_grads():
        for c in range(CHUNKS):
            pltpu.make_async_copy(send.at[X, c, me_e], back_of(c).at[me_e], retown_sem.at[c]).wait()
            scattered(send.at[X, c], back_of(c), ret_send.at[c], ret_recv.at[c]).wait_recv()
        i = iota((1, n_slab_rows), 1)

        def body(j, carry):
            want = jnp.where(((i >> 1) & (OCT - 1)) == j, (i >> 4) * PER + (i & 1), -2)
            total = None
            for c in range(CHUNKS):
                keyc = jnp.where((rank_col >> 1) == c, key_col, -1)
                place = jnp.where(keyc == want, 1.0, 0.0).astype(BF16)
                one = dot(place, back_of(c)[...].reshape(n_slab_rows, oct_w))
                total = one if total is None else total + one
            tok[X, j] = total.astype(BF16)
            return carry

        lax.fori_loop(0, OCT, body, 0)
        copies = [
            pltpu.make_async_copy(
                tok.at[X, j], tg_hbm.at[:, pl.ds(j * oct_w, oct_w)], load_sem.at[0, j]
            )
            for j in range(OCT)
        ]
        for copy in copies:
            copy.start()
        for copy in copies:
            copy.wait()

    build_q(0)
    pl.semaphore_wait(barrier, n_e - 1 + 2)
    for i in range(2):
        swap_weight(i).start()
    for copy in loads[:OCT]:
        copy.wait()
    fill(X, 0)
    dispatch(X, 0)
    for copy in loads[OCT:]:
        copy.wait()
    for j in range(OCT):
        tok[Y, j] = (tok[Y, j].astype(F32) * probs).astype(BF16)
    fill(Y, 0)
    dispatch(Y, 0)
    build_q(1)
    fill(X, 1)
    dispatch(X, 1)
    own(0)
    fill(Y, 1)
    dispatch(Y, 1)
    own_y(0)
    build_q(2)
    for a in (X, Y):
        fill(a, 2)
        dispatch(a, 2)
    arrive(0)
    for copy in weights:
        copy.wait()
    own(1)
    own_y(1)
    complete(0)
    forward(0)
    partial(0)
    arrive(1)
    own(2)
    own_y(2)
    backward(0)
    start_reduce(0)
    complete(1)
    forward(1)
    partial(1)
    arrive(2)
    pass_on(0)
    backward(1)
    start_reduce(1)
    finish(0)
    complete(2)
    forward(2)
    partial(2)
    pass_on(1)
    backward(2)
    start_reduce(2)
    finish(1)
    pass_on(2)
    weight_grads()
    finish(2)
    token_grads()
    for c in range(CHUNKS):
        sent(c)
        dispatched(Y, c).wait_send()
        for i in range(2):
            exchange(c, i).wait_send()
        for way in range(2):
            for slot in range(3):
                toward(c, way, slot).wait_send()
        scattered(send.at[X, c], back_of(c), ret_send.at[c], ret_recv.at[c]).wait_send()
    for i in range(2):
        swap_weight(i).wait_send()


def local(tokens, out_grad, expert_ids, route_probs, w_gate, w_up, w_down):
    n_e = lax.axis_size("expert")
    n_x = lax.axis_size("dp")
    toks, width = tokens.shape
    gate_w, up_w, down_w = w_gate[0], w_up[0], w_down[0]
    quarter = gate_w.shape[1]
    oct_w = width // OCT
    chunk_rows = n_x * n_e * PER
    bw = 512 if width % 512 == 0 else 128
    vmem = pl.BlockSpec(memory_space=pltpu.VMEM)
    hbm = pl.BlockSpec(memory_space=pl.ANY)
    dma = pltpu.SemaphoreType.DMA
    token_grad, gate_grad, up_grad, _ = pl.pallas_call(
        kernel,
        out_shape=(
            jax.ShapeDtypeStruct((toks, width), BF16),
            jax.ShapeDtypeStruct((width, quarter), BF16),
            jax.ShapeDtypeStruct((width, quarter), BF16),
            jax.ShapeDtypeStruct((CHUNKS - 1, 2, 2, n_e, width), BF16),
        ),
        in_specs=[vmem] * 2 + [hbm] * 5,
        out_specs=(hbm, hbm, hbm, hbm),
        scratch_shapes=[
            pltpu.VMEM((2, OCT, toks, oct_w), BF16),
            pltpu.VMEM((max(n_e * SLAB, bw), max(OCT * toks, 4 * quarter)), BF16),
            pltpu.VMEM((width, quarter), BF16),
            pltpu.VMEM((width, quarter), BF16),
            pltpu.VMEM((quarter, width), BF16),
            pltpu.VMEM((2, quarter, width // 2), BF16),
            pltpu.VMEM((2, CHUNKS, n_e, SLAB, oct_w), BF16),
            pltpu.VMEM((2, CHUNKS, n_e, SLAB, oct_w), BF16),
            pltpu.VMEM((2, CHUNKS, 2 * n_x, n_e, width), BF16),
            pltpu.VMEM((CHUNKS, 2, n_e, width), BF16),
            pltpu.VMEM((2, 2, n_e, width), BF16),
            pltpu.VMEM((n_e, SLAB, oct_w), BF16),
            pltpu.VMEM((3, n_x, n_e * PER, quarter), F32),
            pltpu.VMEM((2, 2 * n_e * PER, quarter), F32),
            pltpu.VMEM((CHUNKS, 2, 2 * n_e * PER, quarter), BF16),
            pltpu.VMEM((CHUNKS, 2, 2 * n_e * PER, quarter), BF16),
            pltpu.VMEM((CHUNKS * chunk_rows, 2 * quarter), BF16),
            dma((3, OCT)),
            dma((2, CHUNKS)),
            dma((2, CHUNKS)),
            dma((2, CHUNKS)),
            dma((CHUNKS, 2, 3)),
            dma((CHUNKS, 2, 3)),
            dma((CHUNKS, 2)),
            dma((CHUNKS, 2)),
            dma((2,)),
            dma((2,)),
            dma((CHUNKS, 2)),
            dma((CHUNKS, 2)),
            dma((CHUNKS, 2, 3)),
            dma((CHUNKS, 2, 3)),
            dma((CHUNKS,)),
            dma((CHUNKS,)),
            dma((CHUNKS,)),
            dma((2, 2)),
            dma((2,)),
        ],
        compiler_params=pltpu.CompilerParams(
            collective_id=0, has_side_effects=True, vmem_limit_bytes=127 * 2**19
        ),
    )(
        expert_ids.reshape(1, toks),
        route_probs.reshape(1, toks),
        tokens,
        out_grad,
        gate_w,
        up_w,
        down_w,
    )
    return token_grad, gate_grad[None], up_grad[None]


def solution(mesh):
    in_specs = (
        P(("dp", "expert"), None),
        P(("dp", "expert"), None),
        P(("dp", "expert"), None),
        P(("dp", "expert"), None),
        P("expert", None, "dp"),
        P("expert", None, "dp"),
        P("expert", "dp", None),
    )
    out_specs = (P(("dp", "expert"), None), P("expert", None, "dp"), P("expert", None, "dp"))
    return jax.shard_map(local, mesh=mesh, in_specs=in_specs, out_specs=out_specs, check_vma=False)
```

```python
import jax
import jax.numpy as jnp
from jax import lax
from jax.experimental import pallas as pl
from jax.experimental.pallas import tpu as pltpu
from jax.sharding import PartitionSpec as P

MESH = pl.DeviceIdType.MESH
F32, BF16 = jnp.float32, jnp.bfloat16
CHUNKS = 3
PER = 2
OCT = 8
SLAB = PER * OCT
X, Y = 0, 1
NN = (((1,), (0,)), ((), ()))
NT = (((1,), (1,)), ((), ()))
TN = (((0,), (0,)), ((), ()))


def dot(a, b, dims=NN):
    return lax.dot_general(a, b, dims, preferred_element_type=F32)


def iota(shape, axis):
    return lax.broadcasted_iota(jnp.int32, shape, axis)


def slot_keys(ids_row):
    toks = ids_row.shape[1]
    first, second = iota((toks, toks), 0), iota((toks, toks), 1)
    ids_col = upright(ids_row)
    same = ids_col == ids_row
    rank_row = jnp.sum(jnp.where(same & (first < second), 1, 0), axis=0, keepdims=True)
    rank_col = jnp.sum(jnp.where(same & (second < first), 1, 0), axis=1, keepdims=True)
    return (
        (rank_row, ids_row * PER + (rank_row & 1)),
        (rank_col, ids_col * PER + (rank_col & 1)),
    )


def upright(row):
    toks = row.shape[1]
    eye = iota((toks, toks), 0) == iota((toks, toks), 1)
    return jnp.sum(jnp.where(eye, row, jnp.zeros_like(row)), axis=1, keepdims=True)


def kernel(
    ids_ref, probs_ref, tok_hbm, og_hbm, wg_hbm, wu_hbm, wd_hbm,
    back, gg_hbm, ug_hbm, fin_hbm,
    tok, q, wg, wu, wd, wp, send, recv, rows, relay, fin, acc, part_acc, ex_out, ex_in, grads,
    load_sem, disp_send, disp_recv, own_sem, ag_send, ag_recv, y_send, y_recv, w_send, w_recv,
    ex_send, ex_recv, rs_send, rs_recv, ret_send, ret_recv, retown_sem, out_sem, fin_sem,
):
    n_x = lax.axis_size("dp")
    n_e = lax.axis_size("expert")
    me_x = lax.axis_index("dp")
    me_e = lax.axis_index("expert")
    nbr = (lax.rem(me_x + 1, n_x), lax.rem(me_x + n_x - 1, n_x))
    far = lax.rem(me_x + 2, n_x)
    pair = (me_x + 1 - 2 * lax.rem(me_x, 2), n_x - 1 - me_x)
    toks, width = tok_hbm.shape
    oct_w = width // OCT
    quarter = wg_hbm.shape[1]
    half = n_e
    gs = n_e // 2
    chunk_rows = n_x * n_e * PER
    log_half = half.bit_length() - 1

    loads = []
    for a, src in ((X, tok_hbm), (Y, og_hbm)):
        for j in range(OCT):
            loads.append(
                pltpu.make_async_copy(
                    src.at[:, pl.ds(j * oct_w, oct_w)], tok.at[a, j], load_sem.at[a, j]
                )
            )
            loads[-1].start()
    weights = [
        pltpu.make_async_copy(src, dst, load_sem.at[2, i])
        for i, (src, dst) in enumerate(((wg_hbm, wg), (wu_hbm, wu), (wd_hbm, wd)))
    ]
    for w in weights:
        w.start()

    barrier = pltpu.get_barrier_semaphore()

    def greet(d, carry):
        pl.semaphore_signal(
            barrier, inc=1, device_id=(me_x, lax.rem(me_e + d, n_e)), device_id_type=MESH
        )
        return carry

    lax.fori_loop(1, n_e, greet, 0)
    for x in nbr:
        pl.semaphore_signal(barrier, inc=1, device_id=(x, me_e), device_id_type=MESH)

    (rank_row, key_row), _ = slot_keys(ids_ref[...])
    probs = upright(probs_ref[...])

    n_slab_rows = n_e * SLAB
    step = min(128, n_slab_rows)

    def build_q(c):
        keyc = jnp.where((rank_row >> 1) == c, key_row, -1)
        i = iota((n_slab_rows, 1), 0)
        for j in range(OCT):
            want = jnp.where(((i >> 1) & (OCT - 1)) == j, (i >> 4) * PER + (i & 1), -2)
            q[:n_slab_rows, j * toks : (j + 1) * toks] = jnp.where(want == keyc, 1.0, 0.0).astype(BF16)

    def fill(a, c):
        def body(m, carry):
            part = q[pl.ds(pl.multiple_of(m * step, step), step), : OCT * toks]
            out = dot(part, tok[a].reshape(OCT * toks, oct_w)).astype(BF16)
            send[a, c, pl.ds(m * (step // SLAB), step // SLAB)] = out.reshape(
                step // SLAB, SLAB, oct_w
            )
            return carry

        lax.fori_loop(0, n_slab_rows // step, body, 0)

    def scatter(src, dst, send_sem, recv_sem, self_sem):
        pltpu.make_async_copy(src.at[me_e], dst.at[me_e], self_sem).start()

        def body(d, carry):
            peer = lax.rem(me_e + d, n_e)
            pltpu.make_async_remote_copy(
                src_ref=src.at[peer],
                dst_ref=dst.at[me_e],
                send_sem=send_sem,
                recv_sem=recv_sem,
                device_id=(me_x, peer),
                device_id_type=MESH,
            ).start()
            return carry

        lax.fori_loop(1, n_e, body, 0)

    def scattered(src, dst, send_sem, recv_sem):
        return pltpu.make_async_remote_copy(
            src_ref=src.at[pl.ds(0, n_e - 1)],
            dst_ref=dst.at[pl.ds(0, n_e - 1)],
            send_sem=send_sem,
            recv_sem=recv_sem,
            device_id=(nbr[0], me_e),
            device_id_type=MESH,
        )

    def dispatch(a, c):
        scatter(
            send.at[a, c], recv.at[a, c], disp_send.at[a, c], disp_recv.at[a, c], own_sem.at[a, c]
        )

    def dispatched(a, c):
        return scattered(send.at[a, c], recv.at[a, c], disp_send.at[a, c], disp_recv.at[a, c])

    def hop(a, c, block, h, way, slot):
        ref = rows.at[a, c, block * 2 + h]
        return pltpu.make_async_remote_copy(
            src_ref=ref,
            dst_ref=ref,
            send_sem=ag_send.at[c, way, slot],
            recv_sem=ag_recv.at[c, way, slot],
            device_id=(nbr[way], me_e),
            device_id_type=MESH,
        )

    size = gs * SLAB
    piece = half // 2
    piece_size = size // 2

    def perm(row, col):
        j, rest = row >> log_half, row & (half - 1)
        at = rest >> 1
        slab = (at & (gs // 2 - 1)) * 2 + (at >> (log_half - 2))
        return jnp.where(col == slab * SLAB + j * PER + (rest & 1), 1.0, 0.0).astype(BF16)

    def piece_perm(row, col):
        j, rest = row >> (log_half - 1), row & (piece - 1)
        return jnp.where(col == (rest >> 1) * SLAB + j * PER + (rest & 1), 1.0, 0.0).astype(BF16)

    def collect(a, c):
        pltpu.make_async_copy(send.at[a, c, me_e], recv.at[a, c, me_e], own_sem.at[a, c]).wait()
        dispatched(a, c).wait_recv()
        order = perm(iota((size, size), 0), iota((size, size), 1))
        for h in range(2):
            block = recv[a, c, h * gs : (h + 1) * gs].reshape(size, oct_w)
            out = dot(order, block).astype(BF16)
            for j in range(OCT):
                rows[a, c, me_x * 2 + h, :, j * oct_w : (j + 1) * oct_w] = out[
                    j * half : (j + 1) * half
                ]

    def own(c):
        collect(X, c)
        hop(X, c, me_x, 0, 0, 0).start()
        hop(X, c, me_x, 1, 1, 1).start()
        hop(X, c, me_x, 1, 0, 1).start()
        hop(X, c, me_x, 0, 1, 0).start()

    wide = width // 2

    def swap_weight(i):
        return pltpu.make_async_remote_copy(
            src_ref=wd_hbm.at[:, pl.ds(i * wide, wide)],
            dst_ref=wp.at[i],
            send_sem=w_send.at[i],
            recv_sem=w_recv.at[i],
            device_id=(pair[i], me_e),
            device_id_type=MESH,
        )

    def lend(c, i, block):
        ref = rows.at[Y, c, pl.ds(block * 2, 2), :, pl.ds(i * wide, wide)]
        return pltpu.make_async_remote_copy(
            src_ref=ref,
            dst_ref=ref,
            send_sem=y_send.at[c, i],
            recv_sem=y_recv.at[c, i],
            device_id=(pair[1 - i], me_e),
            device_id_type=MESH,
        )

    def own_y(c):
        collect(Y, c)
        for i in range(2):
            lend(c, i, me_x).start()

    def exchange(c, i):
        return pltpu.make_async_remote_copy(
            src_ref=ex_out.at[c, i],
            dst_ref=ex_in.at[c, i],
            send_sem=ex_send.at[c, i],
            recv_sem=ex_recv.at[c, i],
            device_id=(pair[i], me_e),
            device_id_type=MESH,
        )

    def arrive(c):
        for way in range(2):
            block = nbr[1 - way]
            hop(X, c, block, way, way, way).wait_recv()
            hop(X, c, block, way, way, 2).start()

    def complete(c):
        for way in range(2):
            hop(X, c, nbr[1 - way], 1 - way, way, 1 - way).wait_recv()
            hop(X, c, far, way, way, 2).wait_recv()

    def sent(c):
        for way in range(2):
            for slot in range(2):
                hop(X, c, me_x, slot, way, slot).wait_send()
            hop(X, c, nbr[1 - way], way, way, 2).wait_send()

    kw = width // 4

    def forward(c):
        def body(k, carry):
            cols = pl.ds(pl.multiple_of(k * kw, 128), kw)
            x = rows[X, c, :, :, cols].reshape(chunk_rows, kw)
            g = dot(x, wg[cols, :]).reshape(acc.shape[1:])
            u = dot(x, wu[cols, :]).reshape(acc.shape[1:])

            @pl.when(k == 0)
            def _():
                acc[0] = g
                acc[1] = u

            @pl.when(k > 0)
            def _():
                acc[0] += g
                acc[1] += u

            return carry

        lax.fori_loop(0, 4, body, 0)

    bw = 512 if width % 512 == 0 else 128

    block_rows = 2 * half

    def partial(c):
        for i in range(2):
            lend(c, i, pair[1 - i]).wait_recv()
            if c == 0:
                swap_weight(i).wait_recv()

            def body(k, carry):
                step_w = wide // 4
                near = pl.ds(pl.multiple_of(k * step_w, 128), step_w)
                cols = pl.ds(pl.multiple_of(i * wide + k * step_w, 128), step_w)
                y = jnp.concatenate(
                    [
                        rows[Y, c, pl.ds(p * 2, 2), :, cols].reshape(block_rows, step_w)
                        for p in (me_x, pair[1 - i])
                    ],
                    axis=0,
                )
                mine = dot(y, wd[:, cols], NT)
                lent = dot(y, wp[i, :, near], NT)

                @pl.when(k == 0)
                def _():
                    part_acc[0] = mine
                    part_acc[1] = lent

                @pl.when(k > 0)
                def _():
                    part_acc[0] += mine
                    part_acc[1] += lent

                return carry

            lax.fori_loop(0, 4, body, 0)
            ex_out[c, i] = part_acc[1].astype(BF16)
            exchange(c, i).start()
            if i == 0:
                acc[2, me_x] = part_acc[0, :block_rows]
            else:
                acc[2, me_x] += part_acc[0, :block_rows]
            acc[2, pair[1 - i]] = part_acc[0, block_rows:]

    def backward(c):
        for i in range(2):
            exchange(c, i).wait_recv()
            lend(c, i, me_x).wait_send()
        for i in range(2):
            acc[2, pair[i]] += ex_in[c, i, :block_rows].astype(F32)
        acc[2, far] = ex_in[c, 0, block_rows:].astype(F32) + ex_in[c, 1, block_rows:].astype(F32)
        gate_val, up_val, hidden = (acc[n].reshape(chunk_rows, quarter) for n in range(3))
        s = jax.nn.sigmoid(gate_val)
        grad_up = (hidden * gate_val * s).astype(BF16)
        grad_gate = (hidden * up_val * s * (1.0 + gate_val * (1.0 - s))).astype(BF16)
        grads[c * chunk_rows : (c + 1) * chunk_rows, :quarter] = grad_gate
        grads[c * chunk_rows : (c + 1) * chunk_rows, quarter:] = grad_up

        def part(d, carry):
            cols = pl.ds(pl.multiple_of(d * bw, 128), bw)
            g = grads[c * chunk_rows : (c + 1) * chunk_rows, :quarter]
            u = grads[c * chunk_rows : (c + 1) * chunk_rows, quarter:]
            out = dot(g, wg[cols, :], NT) + dot(u, wu[cols, :], NT)
            rows[Y, c, :, :, cols] = out.astype(BF16).reshape(2 * n_x, half, bw)
            return carry

        lax.fori_loop(0, width // bw, part, 0)

    def last_of(c):
        return fin if c == CHUNKS - 1 else fin_hbm.at[c]

    def toward(c, p, way, slot):
        dst_block = far if slot == 0 else nbr[way]
        h = (way, 1 - way, way)[slot]
        part = pl.ds(p * piece, piece)
        src = rows.at[Y, c, dst_block * 2 + h, part]
        dst = relay.at[c, way, part] if slot == 0 else last_of(c).at[way, h, part]
        return pltpu.make_async_remote_copy(
            src_ref=src,
            dst_ref=dst,
            send_sem=rs_send.at[c, p, way, slot],
            recv_sem=rs_recv.at[c, p, way, slot],
            device_id=(nbr[way], me_e),
            device_id_type=MESH,
        )

    def start_reduce(c):
        for p in range(2):
            for slot in range(2):
                for way in range(2):
                    toward(c, p, way, slot).start()

    def pass_on(c):
        for p in range(2):
            for way in range(2):
                toward(c, p, way, 0).wait_recv()

                def body(d, carry):
                    part = pl.ds(p * piece, piece)
                    cols = pl.ds(pl.multiple_of(d * bw, 128), bw)
                    at = nbr[way] * 2 + way
                    mine = rows[Y, c, at, part, cols].astype(F32)
                    total = mine + relay[c, way, part, cols].astype(F32)
                    rows[Y, c, at, part, cols] = total.astype(BF16)
                    return carry

                lax.fori_loop(0, width // bw, body, 0)
                toward(c, p, way, 2).start()

    def give_back(c, peer):
        pltpu.make_async_remote_copy(
            src_ref=send.at[X, c, peer],
            dst_ref=back.at[c, me_e],
            send_sem=ret_send.at[c],
            recv_sem=ret_recv.at[c],
            device_id=(me_x, peer),
            device_id_type=MESH,
        ).start()

    def finish(c):
        dispatched(X, c).wait_send()
        order = piece_perm(iota((piece_size, piece_size), 1), iota((piece_size, piece_size), 0))
        for p in range(2):
            part = slice(p * piece, (p + 1) * piece)
            for way in range(2):
                for slot in (1, 2):
                    toward(c, p, way, slot).wait_recv()
            for h in range(2):
                if c < CHUNKS - 1:
                    fetch = [
                        pltpu.make_async_copy(
                            fin_hbm.at[c, way, h, pl.ds(p * piece, piece)],
                            relay.at[c, way, pl.ds(p * piece, piece)],
                            fin_sem.at[way],
                        )
                        for way in range(2)
                    ]
                    for copy in fetch:
                        copy.start()
                    for copy in fetch:
                        copy.wait()
                    came = (relay.at[c, 0], relay.at[c, 1])
                else:
                    came = (fin.at[0, h], fin.at[1, h])
                blocks = []
                for j in range(OCT):
                    cols = slice(j * oct_w, (j + 1) * oct_w)
                    total = (
                        rows[Y, c, me_x * 2 + h, part, cols].astype(F32)
                        + came[0][part, cols].astype(F32)
                        + came[1][part, cols].astype(F32)
                    )
                    blocks.append(total.astype(BF16))
                out = dot(order, jnp.concatenate(blocks, axis=0)).astype(BF16)
                for i in range(gs // 2):
                    send[X, c, h * gs + 2 * i + p] = out[i * SLAB : (i + 1) * SLAB]

            def body(d, carry):
                give_back(c, lax.rem(me_e // 2 + d, n_e // 2) * 2 + p)
                return carry

            lax.fori_loop(1, n_e // 2, body, 0)

            @pl.when(lax.rem(me_e, 2) != p)
            def _():
                give_back(c, (me_e // 2) * 2 + p)

        pltpu.make_async_copy(send.at[X, c, me_e], back.at[c, me_e], retown_sem.at[c]).start()

    def stage(slot, o):
        return q.at[pl.ds(0, bw), pl.ds(pl.multiple_of((slot * 2 + o) * quarter, 128), quarter)]

    def weight_grads():
        def tile(i, slot):
            cols = pl.ds(pl.multiple_of(i * bw, 128), bw)
            return [
                pltpu.make_async_copy(stage(slot, o), dst.at[cols, :], out_sem.at[slot, o])
                for o, dst in ((0, gg_hbm), (1, ug_hbm))
            ]

        def body(i, carry):
            slot = lax.rem(i, 2)

            @pl.when(i >= 2)
            def _():
                for copy in tile(i - 2, slot):
                    copy.wait()

            cols = pl.ds(pl.multiple_of(i * bw, 128), bw)
            x = rows[X, :, :, :, cols].reshape(CHUNKS * chunk_rows, bw)
            out = dot(x, grads[...], TN).astype(BF16)
            stage(slot, 0)[...] = out[:, :quarter]
            stage(slot, 1)[...] = out[:, quarter:]
            for copy in tile(i, slot):
                copy.start()
            return carry

        n = width // bw
        lax.fori_loop(0, n, body, 0)
        for i in (n - 2, n - 1):
            for copy in tile(i, i % 2):
                copy.wait()

    build_q(0)
    pl.semaphore_wait(barrier, n_e - 1 + 2)
    for i in range(2):
        swap_weight(i).start()
    for copy in loads[:OCT]:
        copy.wait()
    fill(X, 0)
    dispatch(X, 0)
    for copy in loads[OCT:]:
        copy.wait()
    for j in range(OCT):
        tok[Y, j] = (tok[Y, j].astype(F32) * probs).astype(BF16)
    fill(Y, 0)
    dispatch(Y, 0)
    build_q(1)
    fill(X, 1)
    dispatch(X, 1)
    own(0)
    fill(Y, 1)
    dispatch(Y, 1)
    own_y(0)
    build_q(2)
    for a in (X, Y):
        fill(a, 2)
        dispatch(a, 2)
    arrive(0)
    for copy in weights:
        copy.wait()
    own(1)
    own_y(1)
    complete(0)
    forward(0)
    partial(0)
    arrive(1)
    own(2)
    own_y(2)
    backward(0)
    start_reduce(0)
    complete(1)
    forward(1)
    partial(1)
    arrive(2)
    pass_on(0)
    backward(1)
    start_reduce(1)
    finish(0)
    complete(2)
    forward(2)
    partial(2)
    pass_on(1)
    backward(2)
    start_reduce(2)
    finish(1)
    pass_on(2)
    weight_grads()
    finish(2)
    for c in range(CHUNKS):
        sent(c)
        dispatched(Y, c).wait_send()
        for i in range(2):
            exchange(c, i).wait_send()
        for p in range(2):
            for way in range(2):
                for slot in range(3):
                    toward(c, p, way, slot).wait_send()
        pltpu.make_async_copy(send.at[X, c, me_e], back.at[c, me_e], retown_sem.at[c]).wait()
        scattered(send.at[X, c], back.at[c], ret_send.at[c], ret_recv.at[c]).wait()
    for i in range(2):
        swap_weight(i).wait_send()


def place(ids_ref, back_hbm, gg_src, ug_src, tg_hbm, gg_hbm, ug_hbm, back, out, back_sem, tg_sem, grad_sem):
    width = gg_src.shape[0]
    n_e = back.shape[1]
    oct_w = back.shape[3]
    n_cut = grad_sem.shape[1]
    cut = width // n_cut
    came = [pltpu.make_async_copy(back_hbm.at[c], back.at[c], back_sem.at[c]) for c in range(CHUNKS)]
    moves = [
        pltpu.make_async_copy(
            src.at[pl.ds(i * cut, cut)], dst.at[pl.ds(i * cut, cut)], grad_sem.at[o, i]
        )
        for i in range(n_cut)
        for o, (src, dst) in enumerate(((gg_src, gg_hbm), (ug_src, ug_hbm)))
    ]
    for copy in came + moves:
        copy.start()
    _, (rank_col, key_col) = slot_keys(ids_ref[...])
    i = iota((1, n_e * SLAB), 1)
    for copy in came:
        copy.wait()
    outs = []
    for j in range(OCT):
        want = jnp.where(((i >> 1) & (OCT - 1)) == j, (i >> 4) * PER + (i & 1), -2)
        total = None
        for c in range(CHUNKS):
            keyc = jnp.where((rank_col >> 1) == c, key_col, -1)
            here = jnp.where(keyc == want, 1.0, 0.0).astype(BF16)
            one = dot(here, back[c].reshape(n_e * SLAB, oct_w))
            total = one if total is None else total + one
        out[j] = total.astype(BF16)
        outs.append(
            pltpu.make_async_copy(out.at[j], tg_hbm.at[:, pl.ds(j * oct_w, oct_w)], tg_sem.at[j])
        )
        outs[-1].start()
    for copy in outs + moves:
        copy.wait()


def local(tokens, out_grad, expert_ids, route_probs, w_gate, w_up, w_down):
    n_e = lax.axis_size("expert")
    n_x = lax.axis_size("dp")
    toks, width = tokens.shape
    gate_w, up_w, down_w = w_gate[0], w_up[0], w_down[0]
    quarter = gate_w.shape[1]
    oct_w = width // OCT
    chunk_rows = n_x * n_e * PER
    bw = 512 if width % 512 == 0 else 128
    vmem = pl.BlockSpec(memory_space=pltpu.VMEM)
    hbm = pl.BlockSpec(memory_space=pl.ANY)
    dma = pltpu.SemaphoreType.DMA
    ids_row = expert_ids.reshape(1, toks)
    back, gate_grad, up_grad, _ = pl.pallas_call(
        kernel,
        out_shape=(
            jax.ShapeDtypeStruct((CHUNKS, n_e, SLAB, oct_w), BF16),
            jax.ShapeDtypeStruct((width, quarter), BF16),
            jax.ShapeDtypeStruct((width, quarter), BF16),
            jax.ShapeDtypeStruct((CHUNKS - 1, 2, 2, n_e, width), BF16),
        ),
        in_specs=[vmem] * 2 + [hbm] * 5,
        out_specs=(hbm, hbm, hbm, hbm),
        scratch_shapes=[
            pltpu.VMEM((2, OCT, toks, oct_w), BF16),
            pltpu.VMEM((max(n_e * SLAB, bw), max(OCT * toks, 4 * quarter)), BF16),
            pltpu.VMEM((width, quarter), BF16),
            pltpu.VMEM((width, quarter), BF16),
            pltpu.VMEM((quarter, width), BF16),
            pltpu.VMEM((2, quarter, width // 2), BF16),
            pltpu.VMEM((2, CHUNKS, n_e, SLAB, oct_w), BF16),
            pltpu.VMEM((2, CHUNKS, n_e, SLAB, oct_w), BF16),
            pltpu.VMEM((2, CHUNKS, 2 * n_x, n_e, width), BF16),
            pltpu.VMEM((CHUNKS, 2, n_e, width), BF16),
            pltpu.VMEM((2, 2, n_e, width), BF16),
            pltpu.VMEM((3, n_x, n_e * PER, quarter), F32),
            pltpu.VMEM((2, 2 * n_e * PER, quarter), F32),
            pltpu.VMEM((CHUNKS, 2, 2 * n_e * PER, quarter), BF16),
            pltpu.VMEM((CHUNKS, 2, 2 * n_e * PER, quarter), BF16),
            pltpu.VMEM((CHUNKS * chunk_rows, 2 * quarter), BF16),
            dma((3, OCT)),
            dma((2, CHUNKS)),
            dma((2, CHUNKS)),
            dma((2, CHUNKS)),
            dma((CHUNKS, 2, 3)),
            dma((CHUNKS, 2, 3)),
            dma((CHUNKS, 2)),
            dma((CHUNKS, 2)),
            dma((2,)),
            dma((2,)),
            dma((CHUNKS, 2)),
            dma((CHUNKS, 2)),
            dma((CHUNKS, 2, 2, 3)),
            dma((CHUNKS, 2, 2, 3)),
            dma((CHUNKS,)),
            dma((CHUNKS,)),
            dma((CHUNKS,)),
            dma((2, 2)),
            dma((2,)),
        ],
        compiler_params=pltpu.CompilerParams(
            collective_id=0, has_side_effects=True, vmem_limit_bytes=127 * 2**19
        ),
    )(
        ids_row,
        route_probs.reshape(1, toks),
        tokens,
        out_grad,
        gate_w,
        up_w,
        down_w,
    )
    n_cut = 4
    token_grad, gate_grad, up_grad = pl.pallas_call(
        place,
        out_shape=(
            jax.ShapeDtypeStruct((toks, width), BF16),
            jax.ShapeDtypeStruct((width, quarter), BF16),
            jax.ShapeDtypeStruct((width, quarter), BF16),
        ),
        in_specs=[vmem] + [hbm] * 3,
        out_specs=(hbm, hbm, hbm),
        scratch_shapes=[
            pltpu.VMEM((CHUNKS, n_e, SLAB, oct_w), BF16),
            pltpu.VMEM((OCT, toks, oct_w), BF16),
            dma((CHUNKS,)),
            dma((OCT,)),
            dma((2, n_cut)),
        ],
        compiler_params=pltpu.CompilerParams(vmem_limit_bytes=60 * 2**20),
    )(ids_row, back, gate_grad, up_grad)
    return token_grad, gate_grad[None], up_grad[None]


def solution(mesh):
    in_specs = (
        P(("dp", "expert"), None),
        P(("dp", "expert"), None),
        P(("dp", "expert"), None),
        P(("dp", "expert"), None),
        P("expert", None, "dp"),
        P("expert", None, "dp"),
        P("expert", "dp", None),
    )
    out_specs = (P(("dp", "expert"), None), P("expert", None, "dp"), P("expert", None, "dp"))
    return jax.shard_map(local, mesh=mesh, in_specs=in_specs, out_specs=out_specs, check_vma=False)
```

```python
import jax
import jax.numpy as jnp
from jax import lax
from jax.experimental import pallas as pl
from jax.experimental.pallas import tpu as pltpu
from jax.sharding import PartitionSpec as P

MESH = pl.DeviceIdType.MESH
F32, BF16 = jnp.float32, jnp.bfloat16
CHUNKS = 3
PER = 2
OCT = 8
SLAB = PER * OCT
X, Y, Z = 0, 1, 2
NN = (((1,), (0,)), ((), ()))
NT = (((1,), (1,)), ((), ()))
TN = (((0,), (0,)), ((), ()))


def dot(a, b, dims=NN):
    return lax.dot_general(a, b, dims, preferred_element_type=F32)


def iota(shape, axis):
    return lax.broadcasted_iota(jnp.int32, shape, axis)


def slot_keys(ids_row):
    toks = ids_row.shape[1]
    first, second = iota((toks, toks), 0), iota((toks, toks), 1)
    ids_col = upright(ids_row)
    same = ids_col == ids_row
    rank_row = jnp.sum(jnp.where(same & (first < second), 1, 0), axis=0, keepdims=True)
    rank_col = jnp.sum(jnp.where(same & (second < first), 1, 0), axis=1, keepdims=True)
    return (
        (rank_row, ids_row * PER + (rank_row & 1)),
        (rank_col, ids_col * PER + (rank_col & 1)),
    )


def upright(row):
    toks = row.shape[1]
    eye = iota((toks, toks), 0) == iota((toks, toks), 1)
    return jnp.sum(jnp.where(eye, row, jnp.zeros_like(row)), axis=1, keepdims=True)


def kernel(
    ids_ref, probs_ref, tok_hbm, og_hbm, wg_hbm, wu_hbm, wd_hbm,
    back, gg_hbm, ug_hbm, fin_hbm, recv,
    tok, q, wg, wu, wd, wp, send, slabs, ids_in, probs_in, rows, relay, fin, acc, part_acc, ex_out, ex_in, grads,
    load_sem, disp_send, disp_recv, own_sem, ag_send, ag_recv, og_send, og_recv, meta_send, meta_recv, w_send, w_recv,
    ex_send, ex_recv, rs_send, rs_recv, ret_send, ret_recv, retown_sem, out_sem, fin_sem,
):
    n_x = lax.axis_size("dp")
    n_e = lax.axis_size("expert")
    me_x = lax.axis_index("dp")
    me_e = lax.axis_index("expert")
    nbr = (lax.rem(me_x + 1, n_x), lax.rem(me_x + n_x - 1, n_x))
    far = lax.rem(me_x + 2, n_x)
    pair = (me_x + 1 - 2 * lax.rem(me_x, 2), n_x - 1 - me_x)
    toks, width = tok_hbm.shape
    oct_w = width // OCT
    quarter = wg_hbm.shape[1]
    half = n_e
    gs = n_e // 2
    chunk_rows = n_x * n_e * PER
    log_half = half.bit_length() - 1

    barrier = pltpu.get_barrier_semaphore()

    def greet(d, carry):
        pl.semaphore_signal(
            barrier, inc=1, device_id=(me_x, lax.rem(me_e + d, n_e)), device_id_type=MESH
        )
        return carry

    lax.fori_loop(1, n_e, greet, 0)
    for x in nbr:
        pl.semaphore_signal(barrier, inc=1, device_id=(x, me_e), device_id_type=MESH)

    loads = []
    for a, src in ((X, tok_hbm), (Y, og_hbm)):
        for j in range(OCT):
            loads.append(
                pltpu.make_async_copy(
                    src.at[:, pl.ds(j * oct_w, oct_w)], tok.at[a, j], load_sem.at[a, j]
                )
            )
            loads[-1].start()
    weights = [
        pltpu.make_async_copy(src, dst, load_sem.at[2, i])
        for i, (src, dst) in enumerate(((wg_hbm, wg), (wu_hbm, wu), (wd_hbm, wd)))
    ]
    for w in weights:
        w.start()

    wide = width // 2

    def swap_weight(i):
        return pltpu.make_async_remote_copy(
            src_ref=wd_hbm.at[:, pl.ds(i * wide, wide)],
            dst_ref=wp.at[i],
            send_sem=w_send.at[i],
            recv_sem=w_recv.at[i],
            device_id=(pair[i], me_e),
            device_id_type=MESH,
        )

    def swap(src, dst, i, send_sem, recv_sem):
        return pltpu.make_async_remote_copy(
            src_ref=src,
            dst_ref=dst,
            send_sem=send_sem,
            recv_sem=recv_sem,
            device_id=(pair[1 - i], me_e),
            device_id_type=MESH,
        )

    swaps = []
    for i in range(2):
        for n, (src, dst) in enumerate(((ids_ref, ids_in), (probs_ref, probs_in))):
            swaps.append(swap(src, dst.at[i], i, meta_send.at[i, n], meta_recv.at[i, n]))
    for j in range(OCT // 2):
        for i in range(2):
            at = i * (OCT // 2) + j
            src = og_hbm.at[:, pl.ds(at * oct_w, oct_w)]
            swaps.append(swap(src, tok.at[Z, at], i, og_send.at[at], og_recv.at[at]))

    pl.semaphore_wait(barrier, n_e - 1 + 2)
    for copy in swaps:
        copy.start()
    for i in range(2):
        swap_weight(i).start()

    (rank_row, key_row), _ = slot_keys(ids_ref[...])
    probs = upright(probs_ref[...])

    n_slab_rows = n_e * SLAB
    step = min(256, n_slab_rows)

    def build_q(c, keys=((rank_row, key_row),) * 2):
        i = iota((n_slab_rows, 1), 0)
        for j in range(OCT):
            rank, key = keys[j // (OCT // 2)]
            keyc = jnp.where((rank >> 1) == c, key, -1)
            want = jnp.where(((i >> 1) & (OCT - 1)) == j, (i >> 4) * PER + (i & 1), -2)
            q[:n_slab_rows, j * toks : (j + 1) * toks] = jnp.where(want == keyc, 1.0, 0.0).astype(BF16)

    def fill(a, c):
        def body(m, carry):
            part = q[pl.ds(pl.multiple_of(m * step, step), step), : OCT * toks]
            out = dot(part, tok[a].reshape(OCT * toks, oct_w)).astype(BF16)
            send[a, c, pl.ds(m * (step // SLAB), step // SLAB)] = out.reshape(
                step // SLAB, SLAB, oct_w
            )
            return carry

        lax.fori_loop(0, n_slab_rows // step, body, 0)

    def scatter(src, dst, send_sem, recv_sem, self_sem):
        pltpu.make_async_copy(src.at[me_e], dst.at[me_e], self_sem).start()

        def body(d, carry):
            peer = lax.rem(me_e + d, n_e)
            pltpu.make_async_remote_copy(
                src_ref=src.at[peer],
                dst_ref=dst.at[me_e],
                send_sem=send_sem,
                recv_sem=recv_sem,
                device_id=(me_x, peer),
                device_id_type=MESH,
            ).start()
            return carry

        lax.fori_loop(1, n_e, body, 0)

    def scattered(src, dst, send_sem, recv_sem):
        return pltpu.make_async_remote_copy(
            src_ref=src.at[pl.ds(0, n_e - 1)],
            dst_ref=dst.at[pl.ds(0, n_e - 1)],
            send_sem=send_sem,
            recv_sem=recv_sem,
            device_id=(nbr[0], me_e),
            device_id_type=MESH,
        )

    def dispatch(a, c):
        scatter(
            send.at[a, c], recv.at[a, c], disp_send.at[a, c], disp_recv.at[a, c], own_sem.at[a, c]
        )

    def dispatched(a, c):
        return scattered(send.at[a, c], recv.at[a, c], disp_send.at[a, c], disp_recv.at[a, c])

    def hop(a, c, block, h, way, slot):
        ref = rows.at[a, c, block * 2 + h]
        return pltpu.make_async_remote_copy(
            src_ref=ref,
            dst_ref=ref,
            send_sem=ag_send.at[c, way, slot],
            recv_sem=ag_recv.at[c, way, slot],
            device_id=(nbr[way], me_e),
            device_id_type=MESH,
        )

    size = gs * SLAB
    piece = half // 2
    piece_size = size // 2

    def perm(row, col):
        j, rest = row >> log_half, row & (half - 1)
        at = rest >> 1
        slab = (at & (gs // 2 - 1)) * 2 + (at >> (log_half - 2))
        return jnp.where(col == slab * SLAB + j * PER + (rest & 1), 1.0, 0.0).astype(BF16)

    def piece_perm(row, col):
        j, rest = row >> (log_half - 1), row & (piece - 1)
        return jnp.where(col == (rest >> 1) * SLAB + j * PER + (rest & 1), 1.0, 0.0).astype(BF16)

    def collect(a, c):
        pltpu.make_async_copy(send.at[a, c, me_e], recv.at[a, c, me_e], own_sem.at[a, c]).wait()
        dispatched(a, c).wait_recv()
        load = pltpu.make_async_copy(recv.at[a, c], slabs, own_sem.at[a, c])
        load.start()
        load.wait()
        order = perm(iota((size, size), 0), iota((size, size), 1))
        dst, block_at = (X, me_x) if a == X else (Y, me_x if a == Y else far)
        for h in range(2):
            block = slabs[h * gs : (h + 1) * gs].reshape(size, oct_w)
            out = dot(order, block).astype(BF16)
            for j in range(OCT):
                rows[dst, c, block_at * 2 + h, :, j * oct_w : (j + 1) * oct_w] = out[
                    j * half : (j + 1) * half
                ]

    def own(c):
        collect(X, c)
        hop(X, c, me_x, 0, 0, 0).start()
        hop(X, c, me_x, 1, 1, 1).start()
        hop(X, c, me_x, 1, 0, 1).start()
        hop(X, c, me_x, 0, 1, 0).start()

    def exchange(c, i):
        return pltpu.make_async_remote_copy(
            src_ref=ex_out.at[c, i],
            dst_ref=ex_in.at[c, i],
            send_sem=ex_send.at[c, i],
            recv_sem=ex_recv.at[c, i],
            device_id=(pair[i], me_e),
            device_id_type=MESH,
        )

    def arrive(c):
        for way in range(2):
            block = nbr[1 - way]
            hop(X, c, block, way, way, way).wait_recv()
            hop(X, c, block, way, way, 2).start()

    def complete(c):
        for way in range(2):
            hop(X, c, nbr[1 - way], 1 - way, way, 1 - way).wait_recv()
            hop(X, c, far, way, way, 2).wait_recv()

    def sent(c):
        for way in range(2):
            for slot in range(2):
                hop(X, c, me_x, slot, way, slot).wait_send()
            hop(X, c, nbr[1 - way], way, way, 2).wait_send()

    kw = width // 4

    def forward(c):
        def body(k, carry):
            cols = pl.ds(pl.multiple_of(k * kw, 128), kw)
            x = rows[X, c, :, :, cols].reshape(chunk_rows, kw)
            g = dot(x, wg[cols, :]).reshape(acc.shape[1:])
            u = dot(x, wu[cols, :]).reshape(acc.shape[1:])

            @pl.when(k == 0)
            def _():
                acc[0] = g
                acc[1] = u

            @pl.when(k > 0)
            def _():
                acc[0] += g
                acc[1] += u

            return carry

        lax.fori_loop(0, 4, body, 0)

    bw = 512 if width % 512 == 0 else 128

    block_rows = 2 * half

    def partial(c):
        for i in range(2):
            if c == 0:
                swap_weight(i).wait_recv()

            def body(k, carry):
                step_w = wide // 4
                near = pl.ds(pl.multiple_of(k * step_w, 128), step_w)
                cols = pl.ds(pl.multiple_of(i * wide + k * step_w, 128), step_w)
                y = jnp.concatenate(
                    [
                        rows[Y, c, pl.ds(p * 2, 2), :, cols].reshape(block_rows, step_w)
                        for p in (me_x, far)
                    ],
                    axis=0,
                )
                mine = dot(y, wd[:, cols], NT)
                lent = dot(y, wp[i, :, near], NT)

                @pl.when(k == 0)
                def _():
                    part_acc[0] = mine
                    part_acc[1] = lent

                @pl.when(k > 0)
                def _():
                    part_acc[0] += mine
                    part_acc[1] += lent

                return carry

            lax.fori_loop(0, 4, body, 0)
            ex_out[c, i] = part_acc[1].astype(BF16)
            exchange(c, i).start()
            if i == 0:
                acc[2, me_x] = part_acc[0, :block_rows]
            else:
                acc[2, me_x] += part_acc[0, :block_rows]
            acc[2, pair[1 - i]] = part_acc[0, block_rows:]

    def backward(c):
        for i in range(2):
            exchange(c, i).wait_recv()
        for i in range(2):
            acc[2, pair[i]] += ex_in[c, i, :block_rows].astype(F32)
        acc[2, far] = ex_in[c, 0, block_rows:].astype(F32) + ex_in[c, 1, block_rows:].astype(F32)
        gate_val, up_val, hidden = (acc[n].reshape(chunk_rows, quarter) for n in range(3))
        s = jax.nn.sigmoid(gate_val)
        grad_up = (hidden * gate_val * s).astype(BF16)
        grad_gate = (hidden * up_val * s * (1.0 + gate_val * (1.0 - s))).astype(BF16)
        grads[c * chunk_rows : (c + 1) * chunk_rows, :quarter] = grad_gate
        grads[c * chunk_rows : (c + 1) * chunk_rows, quarter:] = grad_up

        def part(d, carry):
            cols = pl.ds(pl.multiple_of(d * bw, 128), bw)
            g = grads[c * chunk_rows : (c + 1) * chunk_rows, :quarter]
            u = grads[c * chunk_rows : (c + 1) * chunk_rows, quarter:]
            out = dot(g, wg[cols, :], NT) + dot(u, wu[cols, :], NT)
            rows[Y, c, :, :, cols] = out.astype(BF16).reshape(2 * n_x, half, bw)
            return carry

        lax.fori_loop(0, width // bw, part, 0)

    def last_of(c):
        return fin if c == CHUNKS - 1 else fin_hbm.at[c]

    def toward(c, p, way, slot):
        dst_block = far if slot == 0 else nbr[way]
        h = (way, 1 - way, way)[slot]
        part = pl.ds(p * piece, piece)
        src = rows.at[Y, c, dst_block * 2 + h, part]
        dst = relay.at[c, way, part] if slot == 0 else last_of(c).at[way, h, part]
        return pltpu.make_async_remote_copy(
            src_ref=src,
            dst_ref=dst,
            send_sem=rs_send.at[c, p, way, slot],
            recv_sem=rs_recv.at[c, p, way, slot],
            device_id=(nbr[way], me_e),
            device_id_type=MESH,
        )

    def start_reduce(c):
        for p in range(2):
            for slot in range(2):
                for way in range(2):
                    toward(c, p, way, slot).start()

    def pass_on(c):
        for p in range(2):
            for way in range(2):
                toward(c, p, way, 0).wait_recv()

                def body(d, carry):
                    part = pl.ds(p * piece, piece)
                    cols = pl.ds(pl.multiple_of(d * bw, 128), bw)
                    at = nbr[way] * 2 + way
                    mine = rows[Y, c, at, part, cols].astype(F32)
                    total = mine + relay[c, way, part, cols].astype(F32)
                    rows[Y, c, at, part, cols] = total.astype(BF16)
                    return carry

                lax.fori_loop(0, width // bw, body, 0)
                toward(c, p, way, 2).start()

    def give_back(c, peer):
        pltpu.make_async_remote_copy(
            src_ref=send.at[X, c, peer],
            dst_ref=back.at[c, me_e],
            send_sem=ret_send.at[c],
            recv_sem=ret_recv.at[c],
            device_id=(me_x, peer),
            device_id_type=MESH,
        ).start()

    def finish(c):
        dispatched(X, c).wait_send()
        order = piece_perm(iota((piece_size, piece_size), 1), iota((piece_size, piece_size), 0))
        for p in range(2):
            part = slice(p * piece, (p + 1) * piece)
            for way in range(2):
                for slot in (1, 2):
                    toward(c, p, way, slot).wait_recv()
            for h in range(2):
                if c < CHUNKS - 1:
                    fetch = [
                        pltpu.make_async_copy(
                            fin_hbm.at[c, way, h, pl.ds(p * piece, piece)],
                            relay.at[c, way, pl.ds(p * piece, piece)],
                            fin_sem.at[way],
                        )
                        for way in range(2)
                    ]
                    for copy in fetch:
                        copy.start()
                    for copy in fetch:
                        copy.wait()
                    came = (relay.at[c, 0], relay.at[c, 1])
                else:
                    came = (fin.at[0, h], fin.at[1, h])
                blocks = []
                for j in range(OCT):
                    cols = slice(j * oct_w, (j + 1) * oct_w)
                    total = (
                        rows[Y, c, me_x * 2 + h, part, cols].astype(F32)
                        + came[0][part, cols].astype(F32)
                        + came[1][part, cols].astype(F32)
                    )
                    blocks.append(total.astype(BF16))
                out = dot(order, jnp.concatenate(blocks, axis=0)).astype(BF16)
                for i in range(gs // 2):
                    send[X, c, h * gs + 2 * i + p] = out[i * SLAB : (i + 1) * SLAB]

            def body(d, carry):
                give_back(c, lax.rem(me_e // 2 + d, n_e // 2) * 2 + p)
                return carry

            lax.fori_loop(1, n_e // 2, body, 0)

            @pl.when(lax.rem(me_e, 2) != p)
            def _():
                give_back(c, (me_e // 2) * 2 + p)

        pltpu.make_async_copy(send.at[X, c, me_e], back.at[c, me_e], retown_sem.at[c]).start()

    def stage(slot, o):
        return q.at[pl.ds(0, bw), pl.ds(pl.multiple_of((slot * 2 + o) * quarter, 128), quarter)]

    def weight_grads():
        def tile(i, slot):
            cols = pl.ds(pl.multiple_of(i * bw, 128), bw)
            return [
                pltpu.make_async_copy(stage(slot, o), dst.at[cols, :], out_sem.at[slot, o])
                for o, dst in ((0, gg_hbm), (1, ug_hbm))
            ]

        def body(i, carry):
            slot = lax.rem(i, 2)

            @pl.when(i >= 2)
            def _():
                for copy in tile(i - 2, slot):
                    copy.wait()

            cols = pl.ds(pl.multiple_of(i * bw, 128), bw)
            x = rows[X, :, :, :, cols].reshape(CHUNKS * chunk_rows, bw)
            out = dot(x, grads[...], TN).astype(BF16)
            stage(slot, 0)[...] = out[:, :quarter]
            stage(slot, 1)[...] = out[:, quarter:]
            for copy in tile(i, slot):
                copy.start()
            return carry

        n = width // bw
        lax.fori_loop(0, n, body, 0)
        for i in (n - 2, n - 1):
            for copy in tile(i, i % 2):
                copy.wait()

    def fill_out(a, c):
        fill(a, c)
        dispatch(a, c)

    build_q(0)
    for copy in loads[:OCT]:
        copy.wait()
    fill_out(X, 0)
    for copy in loads[OCT:]:
        copy.wait()
    for j in range(OCT):
        tok[Y, j] = (tok[Y, j].astype(F32) * probs).astype(BF16)
    fill_out(Y, 0)
    build_q(1)
    fill_out(X, 1)
    fill_out(Y, 1)
    for copy in swaps:
        copy.wait_recv()
    partner_keys = tuple(slot_keys(ids_in[i])[0] for i in range(2))
    for j in range(OCT):
        scale = upright(probs_in[j // (OCT // 2)])
        tok[Z, j] = (tok[Z, j].astype(F32) * scale).astype(BF16)
    build_q(0, partner_keys)
    fill_out(Z, 0)
    own(0)
    build_q(2)
    fill_out(X, 2)
    build_q(1, partner_keys)
    fill_out(Z, 1)
    build_q(2)
    fill_out(Y, 2)
    build_q(2, partner_keys)
    fill_out(Z, 2)
    collect(Y, 0)
    for copy in weights:
        copy.wait()
    own(1)
    collect(Z, 0)
    arrive(0)
    collect(Y, 1)
    partial(0)
    own(2)
    arrive(1)
    complete(0)
    forward(0)
    backward(0)
    start_reduce(0)
    collect(Z, 1)
    partial(1)
    arrive(2)
    complete(1)
    forward(1)
    pass_on(0)
    backward(1)
    start_reduce(1)
    collect(Y, 2)
    collect(Z, 2)
    partial(2)
    finish(0)
    complete(2)
    forward(2)
    pass_on(1)
    backward(2)
    start_reduce(2)
    finish(1)
    pass_on(2)
    weight_grads()
    finish(2)
    for c in range(CHUNKS):
        sent(c)
        for a in (Y, Z):
            dispatched(a, c).wait_send()
        for i in range(2):
            exchange(c, i).wait_send()
        for p in range(2):
            for way in range(2):
                for slot in range(3):
                    toward(c, p, way, slot).wait_send()
        pltpu.make_async_copy(send.at[X, c, me_e], back.at[c, me_e], retown_sem.at[c]).wait()
        scattered(send.at[X, c], back.at[c], ret_send.at[c], ret_recv.at[c]).wait()
    for i in range(2):
        swap_weight(i).wait_send()
    for copy in swaps:
        copy.wait_send()


def place(ids_ref, back_hbm, gg_src, ug_src, tg_hbm, gg_hbm, ug_hbm, back, rows, out, grad, back_sem, tg_sem, in_sem, out_sem):
    width = gg_src.shape[0]
    n_e = back.shape[1]
    oct_w = back.shape[3]
    cut = width // (OCT // 2)
    came = [pltpu.make_async_copy(back_hbm.at[c], back.at[c], back_sem.at[c]) for c in range(CHUNKS)]
    moves = []
    for j in range(OCT):
        o, at = j % 2, pl.ds((j // 2) * cut, cut)
        src, dst = ((gg_src, gg_hbm), (ug_src, ug_hbm))[o]
        moves.append(
            (
                pltpu.make_async_copy(src.at[at], grad.at[o, at], in_sem.at[j]),
                pltpu.make_async_copy(grad.at[o, at], dst.at[at], out_sem.at[j]),
            )
        )
    for copy in came:
        copy.start()
    for copy, _ in moves:
        copy.start()
    _, (rank_col, key_col) = slot_keys(ids_ref[...])
    half = n_e // 2 * SLAB
    per_half = n_e // 2 * PER
    slot, col = iota((half, half), 0), iota((half, half), 1)
    j, rest = slot // per_half, slot % per_half
    order = jnp.where(col == (rest // PER) * SLAB + j * PER + rest % PER, 1.0, 0.0).astype(BF16)
    at = (rank_col // PER) * (n_e * PER) + key_col
    here = jnp.where(at == iota((1, CHUNKS * n_e * PER), 1), 1.0, 0.0).astype(BF16)
    for c in range(CHUNKS):
        came[c].wait()
        for h in range(2):
            block = back[c, h * (n_e // 2) : (h + 1) * (n_e // 2)].reshape(half, oct_w)
            flat = dot(order, block).astype(BF16)
            first = c * n_e * PER + h * per_half
            for j in range(OCT):
                rows[first : first + per_half, j * oct_w : (j + 1) * oct_w] = flat[
                    j * per_half : (j + 1) * per_half
                ]
    outs = []
    for j in range(OCT):
        out[j] = dot(here, rows[:, j * oct_w : (j + 1) * oct_w]).astype(BF16)
        outs.append(
            pltpu.make_async_copy(out.at[j], tg_hbm.at[:, pl.ds(j * oct_w, oct_w)], tg_sem.at[j])
        )
        outs[-1].start()
        moves[j][0].wait()
        moves[j][1].start()
    for copy in outs:
        copy.wait()
    for _, copy in moves:
        copy.wait()


def local(tokens, out_grad, expert_ids, route_probs, w_gate, w_up, w_down):
    n_e = lax.axis_size("expert")
    n_x = lax.axis_size("dp")
    toks, width = tokens.shape
    gate_w, up_w, down_w = w_gate[0], w_up[0], w_down[0]
    quarter = gate_w.shape[1]
    oct_w = width // OCT
    chunk_rows = n_x * n_e * PER
    bw = 512 if width % 512 == 0 else 128
    vmem = pl.BlockSpec(memory_space=pltpu.VMEM)
    hbm = pl.BlockSpec(memory_space=pl.ANY)
    dma = pltpu.SemaphoreType.DMA
    ids_row = expert_ids.reshape(1, toks)
    back, gate_grad, up_grad, _, _ = pl.pallas_call(
        kernel,
        out_shape=(
            jax.ShapeDtypeStruct((CHUNKS, n_e, SLAB, oct_w), BF16),
            jax.ShapeDtypeStruct((width, quarter), BF16),
            jax.ShapeDtypeStruct((width, quarter), BF16),
            jax.ShapeDtypeStruct((CHUNKS - 1, 2, 2, n_e, width), BF16),
            jax.ShapeDtypeStruct((3, CHUNKS, n_e, SLAB, oct_w), BF16),
        ),
        in_specs=[vmem] * 2 + [hbm] * 5,
        out_specs=(hbm,) * 5,
        scratch_shapes=[
            pltpu.VMEM((3, OCT, toks, oct_w), BF16),
            pltpu.VMEM((max(n_e * SLAB, bw), max(OCT * toks, 4 * quarter)), BF16),
            pltpu.VMEM((width, quarter), BF16),
            pltpu.VMEM((width, quarter), BF16),
            pltpu.VMEM((quarter, width), BF16),
            pltpu.VMEM((2, quarter, width // 2), BF16),
            pltpu.VMEM((3, CHUNKS, n_e, SLAB, oct_w), BF16),
            pltpu.VMEM((n_e, SLAB, oct_w), BF16),
            pltpu.VMEM((2, 1, toks), jnp.int32),
            pltpu.VMEM((2, 1, toks), F32),
            pltpu.VMEM((2, CHUNKS, 2 * n_x, n_e, width), BF16),
            pltpu.VMEM((CHUNKS, 2, n_e, width), BF16),
            pltpu.VMEM((2, 2, n_e, width), BF16),
            pltpu.VMEM((3, n_x, n_e * PER, quarter), F32),
            pltpu.VMEM((2, 2 * n_e * PER, quarter), F32),
            pltpu.VMEM((CHUNKS, 2, 2 * n_e * PER, quarter), BF16),
            pltpu.VMEM((CHUNKS, 2, 2 * n_e * PER, quarter), BF16),
            pltpu.VMEM((CHUNKS * chunk_rows, 2 * quarter), BF16),
            dma((3, OCT)),
            dma((3, CHUNKS)),
            dma((3, CHUNKS)),
            dma((3, CHUNKS)),
            dma((CHUNKS, 2, 3)),
            dma((CHUNKS, 2, 3)),
            dma((OCT,)),
            dma((OCT,)),
            dma((2, 2)),
            dma((2, 2)),
            dma((2,)),
            dma((2,)),
            dma((CHUNKS, 2)),
            dma((CHUNKS, 2)),
            dma((CHUNKS, 2, 2, 3)),
            dma((CHUNKS, 2, 2, 3)),
            dma((CHUNKS,)),
            dma((CHUNKS,)),
            dma((CHUNKS,)),
            dma((2, 2)),
            dma((2,)),
        ],
        compiler_params=pltpu.CompilerParams(
            collective_id=0, has_side_effects=True, vmem_limit_bytes=127 * 2**19
        ),
    )(
        ids_row,
        route_probs.reshape(1, toks),
        tokens,
        out_grad,
        gate_w,
        up_w,
        down_w,
    )
    token_grad, gate_grad, up_grad = pl.pallas_call(
        place,
        out_shape=(
            jax.ShapeDtypeStruct((toks, width), BF16),
            jax.ShapeDtypeStruct((width, quarter), BF16),
            jax.ShapeDtypeStruct((width, quarter), BF16),
        ),
        in_specs=[vmem] + [hbm] * 3,
        out_specs=(hbm, hbm, hbm),
        scratch_shapes=[
            pltpu.VMEM((CHUNKS, n_e, SLAB, oct_w), BF16),
            pltpu.VMEM((CHUNKS * n_e * PER, width), BF16),
            pltpu.VMEM((OCT, toks, oct_w), BF16),
            pltpu.VMEM((2, width, quarter), BF16),
            dma((CHUNKS,)),
            dma((OCT,)),
            dma((OCT,)),
            dma((OCT,)),
        ],
        compiler_params=pltpu.CompilerParams(vmem_limit_bytes=60 * 2**20),
    )(ids_row, back, gate_grad, up_grad)
    return token_grad, gate_grad[None], up_grad[None]


def solution(mesh):
    in_specs = (
        P(("dp", "expert"), None),
        P(("dp", "expert"), None),
        P(("dp", "expert"), None),
        P(("dp", "expert"), None),
        P("expert", None, "dp"),
        P("expert", None, "dp"),
        P("expert", "dp", None),
    )
    out_specs = (P(("dp", "expert"), None), P("expert", None, "dp"), P("expert", None, "dp"))
    return jax.shard_map(local, mesh=mesh, in_specs=in_specs, out_specs=out_specs, check_vma=False)
```

```python
import jax
import jax.numpy as jnp
from jax import lax
from jax.experimental import pallas as pl
from jax.experimental.pallas import tpu as pltpu
from jax.sharding import PartitionSpec as P

MESH = pl.DeviceIdType.MESH
F32, BF16 = jnp.float32, jnp.bfloat16
CHUNKS = 3
PER = 2
OCT = 8
SLAB = PER * OCT
X, Y, Z, V = 0, 1, 2, 3
SOURCE = (0, 0, 1, 2)
NN = (((1,), (0,)), ((), ()))
NT = (((1,), (1,)), ((), ()))
TN = (((0,), (0,)), ((), ()))


def dot(a, b, dims=NN):
    return lax.dot_general(a, b, dims, preferred_element_type=F32)


def iota(shape, axis):
    return lax.broadcasted_iota(jnp.int32, shape, axis)


def slot_keys(ids_row):
    toks = ids_row.shape[1]
    first, second = iota((toks, toks), 0), iota((toks, toks), 1)
    ids_col = upright(ids_row)
    same = ids_col == ids_row
    rank_row = jnp.sum(jnp.where(same & (first < second), 1, 0), axis=0, keepdims=True)
    rank_col = jnp.sum(jnp.where(same & (second < first), 1, 0), axis=1, keepdims=True)
    return (
        (rank_row, ids_row * PER + (rank_row & 1)),
        (rank_col, ids_col * PER + (rank_col & 1)),
    )


def upright(row):
    toks = row.shape[1]
    eye = iota((toks, toks), 0) == iota((toks, toks), 1)
    return jnp.sum(jnp.where(eye, row, jnp.zeros_like(row)), axis=1, keepdims=True)


def kernel(
    ids_ref, probs_ref, tok_hbm, og_hbm, wg_hbm, wu_hbm, wd_hbm,
    back, gg_hbm, ug_hbm, fin_hbm, recv,
    tok, q, wg, wu, wd, wp, send, slabs, ids_in, probs_in, rows, relay, fin, acc, part_acc, ex_out, ex_in, grads,
    load_sem, disp_send, disp_recv, own_sem, ag_send, ag_recv, raw_send, raw_recv, meta_send, meta_recv, w_send, w_recv,
    ex_send, ex_recv, rs_send, rs_recv, ret_send, ret_recv, retown_sem, out_sem, fin_sem,
):
    n_x = lax.axis_size("dp")
    n_e = lax.axis_size("expert")
    me_x = lax.axis_index("dp")
    me_e = lax.axis_index("expert")
    nbr = (lax.rem(me_x + 1, n_x), lax.rem(me_x + n_x - 1, n_x))
    far = lax.rem(me_x + 2, n_x)
    pair = (me_x + 1 - 2 * lax.rem(me_x, 2), n_x - 1 - me_x)
    toks, width = tok_hbm.shape
    oct_w = width // OCT
    quarter = wg_hbm.shape[1]
    half = n_e
    gs = n_e // 2
    chunk_rows = n_x * n_e * PER
    log_half = half.bit_length() - 1

    barrier = pltpu.get_barrier_semaphore()

    def greet(d, carry):
        pl.semaphore_signal(
            barrier, inc=1, device_id=(me_x, lax.rem(me_e + d, n_e)), device_id_type=MESH
        )
        return carry

    lax.fori_loop(1, n_e, greet, 0)
    for x in nbr:
        pl.semaphore_signal(barrier, inc=1, device_id=(x, me_e), device_id_type=MESH)

    loads = [
        pltpu.make_async_copy(
            src.at[:, pl.ds(j * oct_w, oct_w)], tok.at[SOURCE[a], j], load_sem.at[a, j]
        )
        for a, src in ((X, tok_hbm), (Y, og_hbm))
        for j in range(OCT)
    ]
    for copy in loads[:OCT]:
        copy.start()
    weights = [
        pltpu.make_async_copy(src, dst, load_sem.at[2, i])
        for i, (src, dst) in enumerate(((wg_hbm, wg), (wu_hbm, wu), (wd_hbm, wd)))
    ]
    for w in weights:
        w.start()

    wide = width // 2

    def swap_weight(i):
        return pltpu.make_async_remote_copy(
            src_ref=wd_hbm.at[:, pl.ds(i * wide, wide)],
            dst_ref=wp.at[i],
            send_sem=w_send.at[i],
            recv_sem=w_recv.at[i],
            device_id=(pair[i], me_e),
            device_id_type=MESH,
        )

    def swap(src, dst, i, send_sem, recv_sem):
        return pltpu.make_async_remote_copy(
            src_ref=src,
            dst_ref=dst,
            send_sem=send_sem,
            recv_sem=recv_sem,
            device_id=(pair[1 - i], me_e),
            device_id_type=MESH,
        )

    swaps = []
    for i in range(2):
        for n, (src, dst) in enumerate(((ids_ref, ids_in), (probs_ref, probs_in))):
            swaps.append(swap(src, dst.at[i], i, meta_send.at[i, n], meta_recv.at[i, n]))
    for a, whole in ((V, tok_hbm), (Z, og_hbm)):
        for j in range(OCT // 2):
            for i in range(2):
                at = i * (OCT // 2) + j
                src = whole.at[:, pl.ds(at * oct_w, oct_w)]
                n = a - Z
                dst = tok.at[SOURCE[a], at]
                swaps.append(swap(src, dst, i, raw_send.at[n, at], raw_recv.at[n, at]))
    first_cotangent = len(swaps) - OCT

    pl.semaphore_wait(barrier, n_e - 1 + 2)
    for copy in swaps:
        copy.start()
    for i in range(2):
        swap_weight(i).start()

    (rank_row, key_row), _ = slot_keys(ids_ref[...])
    probs = upright(probs_ref[...])

    n_slab_rows = n_e * SLAB
    step = min(256, n_slab_rows)

    def build_q(c, keys=((rank_row, key_row),) * 2):
        for part, (rank, key) in enumerate(keys):

            def body(j, carry):
                keyc = jnp.where((rank >> 1) == c, key, -1)
                i = iota((n_slab_rows, 1), 0)
                want = jnp.where(((i >> 1) & (OCT - 1)) == j, (i >> 4) * PER + (i & 1), -2)
                cols = pl.ds(pl.multiple_of(j * toks, toks), toks)
                q[:n_slab_rows, cols] = jnp.where(want == keyc, 1.0, 0.0).astype(BF16)
                return carry

            lax.fori_loop(part * (OCT // 2), (part + 1) * (OCT // 2), body, 0)

    def slab_of(a, c):
        return send.at[((Y, 2), (Z, 1), (Z, 2))[c] if a == V else (a, c)]

    def fill(a, c):
        def body(m, carry):
            part = q[pl.ds(pl.multiple_of(m * step, step), step), : OCT * toks]
            out = dot(part, tok[SOURCE[a]].reshape(OCT * toks, oct_w)).astype(BF16)
            slab_of(a, c)[pl.ds(m * (step // SLAB), step // SLAB)] = out.reshape(
                step // SLAB, SLAB, oct_w
            )
            return carry

        lax.fori_loop(0, n_slab_rows // step, body, 0)

    def scatter(src, dst, send_sem, recv_sem, self_sem):
        pltpu.make_async_copy(src.at[me_e], dst.at[me_e], self_sem).start()

        def body(d, carry):
            peer = lax.rem(me_e + d, n_e)
            pltpu.make_async_remote_copy(
                src_ref=src.at[peer],
                dst_ref=dst.at[me_e],
                send_sem=send_sem,
                recv_sem=recv_sem,
                device_id=(me_x, peer),
                device_id_type=MESH,
            ).start()
            return carry

        lax.fori_loop(1, n_e, body, 0)

    def scattered(src, dst, send_sem, recv_sem):
        return pltpu.make_async_remote_copy(
            src_ref=src.at[pl.ds(0, n_e - 1)],
            dst_ref=dst.at[pl.ds(0, n_e - 1)],
            send_sem=send_sem,
            recv_sem=recv_sem,
            device_id=(nbr[0], me_e),
            device_id_type=MESH,
        )

    def dispatch(a, c):
        scatter(
            slab_of(a, c), recv.at[a, c], disp_send.at[a, c], disp_recv.at[a, c], own_sem.at[a, c]
        )

    def dispatched(a, c):
        return scattered(slab_of(a, c), recv.at[a, c], disp_send.at[a, c], disp_recv.at[a, c])

    def share(c, i, n, block):
        ref = rows.at[X, c, pl.ds(block * 2, 2), :, pl.ds(i * wide, wide)]
        return pltpu.make_async_remote_copy(
            src_ref=ref,
            dst_ref=ref,
            send_sem=ag_send.at[c, i, n],
            recv_sem=ag_recv.at[c, i, n],
            device_id=(pair[i], me_e),
            device_id_type=MESH,
        )

    size = gs * SLAB
    piece = half // 2
    piece_size = size // 2

    def perm(row, col):
        j, rest = row >> log_half, row & (half - 1)
        at = rest >> 1
        slab = (at & (gs // 2 - 1)) * 2 + (at >> (log_half - 2))
        return jnp.where(col == slab * SLAB + j * PER + (rest & 1), 1.0, 0.0).astype(BF16)

    def piece_perm(row, col):
        j, rest = row >> (log_half - 1), row & (piece - 1)
        return jnp.where(col == (rest >> 1) * SLAB + j * PER + (rest & 1), 1.0, 0.0).astype(BF16)

    def collect(a, c):
        pltpu.make_async_copy(slab_of(a, c).at[me_e], recv.at[a, c, me_e], own_sem.at[a, c]).wait()
        dispatched(a, c).wait_recv()
        load = pltpu.make_async_copy(recv.at[a, c], slabs, own_sem.at[a, c])
        load.start()
        load.wait()
        order = perm(iota((size, size), 0), iota((size, size), 1))
        dst = X if a in (X, V) else Y
        block_at = {X: (me_x, me_x), Y: (me_x, me_x), Z: (far, far), V: (pair[1], pair[0])}[a]
        for h in range(2):
            block = slabs[h * gs : (h + 1) * gs].reshape(size, oct_w)
            out = dot(order, block).astype(BF16)
            for j in range(OCT):
                rows[
                    dst, c, block_at[j // (OCT // 2)] * 2 + h, :, j * oct_w : (j + 1) * oct_w
                ] = out[
                    j * half : (j + 1) * half
                ]

    def own(c):
        collect(X, c)
        for i in range(2):
            share(c, i, 0, me_x).start()

    def lent(c):
        collect(V, c)
        for i in range(2):
            share(c, i, 1, pair[1 - i]).start()

    def exchange(c, i):
        return pltpu.make_async_remote_copy(
            src_ref=ex_out.at[c, i],
            dst_ref=ex_in.at[c, i],
            send_sem=ex_send.at[c, i],
            recv_sem=ex_recv.at[c, i],
            device_id=(pair[i], me_e),
            device_id_type=MESH,
        )

    def complete(c):
        for i in range(2):
            share(c, i, 0, pair[i]).wait_recv()
            share(c, i, 1, far).wait_recv()

    def sent(c):
        for i in range(2):
            share(c, i, 0, me_x).wait_send()
            share(c, i, 1, pair[1 - i]).wait_send()

    kw = width // 4

    def forward(c):
        def body(k, carry):
            cols = pl.ds(pl.multiple_of(k * kw, 128), kw)
            x = rows[X, c, :, :, cols].reshape(chunk_rows, kw)
            g = dot(x, wg[cols, :]).reshape(acc.shape[1:])
            u = dot(x, wu[cols, :]).reshape(acc.shape[1:])

            @pl.when(k == 0)
            def _():
                acc[0] = g
                acc[1] = u

            @pl.when(k > 0)
            def _():
                acc[0] += g
                acc[1] += u

            return carry

        lax.fori_loop(0, 4, body, 0)

    bw = 512 if width % 512 == 0 else 128

    block_rows = 2 * half

    def partial(c):
        for i in range(2):
            if c == 0:
                swap_weight(i).wait_recv()

            def body(k, carry):
                step_w = wide // 4
                near = pl.ds(pl.multiple_of(k * step_w, 128), step_w)
                cols = pl.ds(pl.multiple_of(i * wide + k * step_w, 128), step_w)
                y = jnp.concatenate(
                    [
                        rows[Y, c, pl.ds(p * 2, 2), :, cols].reshape(block_rows, step_w)
                        for p in (me_x, far)
                    ],
                    axis=0,
                )
                mine = dot(y, wd[:, cols], NT)
                other = dot(y, wp[i, :, near], NT)

                @pl.when(k == 0)
                def _():
                    part_acc[0] = mine
                    part_acc[1] = other

                @pl.when(k > 0)
                def _():
                    part_acc[0] += mine
                    part_acc[1] += other

                return carry

            lax.fori_loop(0, 4, body, 0)
            ex_out[c, i] = part_acc[1].astype(BF16)
            exchange(c, i).start()
            if i == 0:
                acc[2, me_x] = part_acc[0, :block_rows]
            else:
                acc[2, me_x] += part_acc[0, :block_rows]
            acc[2, pair[1 - i]] = part_acc[0, block_rows:]

    def backward(c):
        for i in range(2):
            exchange(c, i).wait_recv()
        for i in range(2):
            acc[2, pair[i]] += ex_in[c, i, :block_rows].astype(F32)
        acc[2, far] = ex_in[c, 0, block_rows:].astype(F32) + ex_in[c, 1, block_rows:].astype(F32)
        gate_val, up_val, hidden = (acc[n].reshape(chunk_rows, quarter) for n in range(3))
        s = jax.nn.sigmoid(gate_val)
        grad_up = (hidden * gate_val * s).astype(BF16)
        grad_gate = (hidden * up_val * s * (1.0 + gate_val * (1.0 - s))).astype(BF16)
        grads[c * chunk_rows : (c + 1) * chunk_rows, :quarter] = grad_gate
        grads[c * chunk_rows : (c + 1) * chunk_rows, quarter:] = grad_up

        def part(d, carry):
            cols = pl.ds(pl.multiple_of(d * bw, 128), bw)
            g = grads[c * chunk_rows : (c + 1) * chunk_rows, :quarter]
            u = grads[c * chunk_rows : (c + 1) * chunk_rows, quarter:]
            out = dot(g, wg[cols, :], NT) + dot(u, wu[cols, :], NT)
            rows[Y, c, :, :, cols] = out.astype(BF16).reshape(2 * n_x, half, bw)
            return carry

        lax.fori_loop(0, width // bw, part, 0)

    def last_of(c):
        return fin if c == CHUNKS - 1 else fin_hbm.at[c]

    def toward(c, p, way, slot):
        dst_block = far if slot == 0 else nbr[way]
        h = (way, 1 - way, way)[slot]
        part = pl.ds(p * piece, piece)
        src = rows.at[Y, c, dst_block * 2 + h, part]
        dst = relay.at[c, way, part] if slot == 0 else last_of(c).at[way, h, part]
        return pltpu.make_async_remote_copy(
            src_ref=src,
            dst_ref=dst,
            send_sem=rs_send.at[c, p, way, slot],
            recv_sem=rs_recv.at[c, p, way, slot],
            device_id=(nbr[way], me_e),
            device_id_type=MESH,
        )

    def start_reduce(c):
        for p in range(2):
            for slot in range(2):
                for way in range(2):
                    toward(c, p, way, slot).start()

    def pass_on(c):
        for p in range(2):
            for way in range(2):
                toward(c, p, way, 0).wait_recv()

                def body(d, carry):
                    part = pl.ds(p * piece, piece)
                    cols = pl.ds(pl.multiple_of(d * bw, 128), bw)
                    at = nbr[way] * 2 + way
                    mine = rows[Y, c, at, part, cols].astype(F32)
                    total = mine + relay[c, way, part, cols].astype(F32)
                    rows[Y, c, at, part, cols] = total.astype(BF16)
                    return carry

                lax.fori_loop(0, width // bw, body, 0)
                toward(c, p, way, 2).start()

    def give_back(c, peer):
        pltpu.make_async_remote_copy(
            src_ref=send.at[X, c, peer],
            dst_ref=back.at[c, me_e],
            send_sem=ret_send.at[c],
            recv_sem=ret_recv.at[c],
            device_id=(me_x, peer),
            device_id_type=MESH,
        ).start()

    def finish(c):
        dispatched(X, c).wait_send()
        order = piece_perm(iota((piece_size, piece_size), 1), iota((piece_size, piece_size), 0))
        for p in range(2):
            part = slice(p * piece, (p + 1) * piece)
            for way in range(2):
                for slot in (1, 2):
                    toward(c, p, way, slot).wait_recv()
            for h in range(2):
                if c < CHUNKS - 1:
                    fetch = [
                        pltpu.make_async_copy(
                            fin_hbm.at[c, way, h, pl.ds(p * piece, piece)],
                            relay.at[c, way, pl.ds(p * piece, piece)],
                            fin_sem.at[way],
                        )
                        for way in range(2)
                    ]
                    for copy in fetch:
                        copy.start()
                    for copy in fetch:
                        copy.wait()
                    came = (relay.at[c, 0], relay.at[c, 1])
                else:
                    came = (fin.at[0, h], fin.at[1, h])
                blocks = []
                for j in range(OCT):
                    cols = slice(j * oct_w, (j + 1) * oct_w)
                    total = (
                        rows[Y, c, me_x * 2 + h, part, cols].astype(F32)
                        + came[0][part, cols].astype(F32)
                        + came[1][part, cols].astype(F32)
                    )
                    blocks.append(total.astype(BF16))
                out = dot(order, jnp.concatenate(blocks, axis=0)).astype(BF16)
                for i in range(gs // 2):
                    send[X, c, h * gs + 2 * i + p] = out[i * SLAB : (i + 1) * SLAB]

            def body(d, carry):
                give_back(c, lax.rem(me_e // 2 + d, n_e // 2) * 2 + p)
                return carry

            lax.fori_loop(1, n_e // 2, body, 0)

            @pl.when(lax.rem(me_e, 2) != p)
            def _():
                give_back(c, (me_e // 2) * 2 + p)

        pltpu.make_async_copy(send.at[X, c, me_e], back.at[c, me_e], retown_sem.at[c]).start()

    def stage(slot, o):
        return q.at[pl.ds(0, bw), pl.ds(pl.multiple_of((slot * 2 + o) * quarter, 128), quarter)]

    def weight_grads():
        def tile(i, slot):
            cols = pl.ds(pl.multiple_of(i * bw, 128), bw)
            return [
                pltpu.make_async_copy(stage(slot, o), dst.at[cols, :], out_sem.at[slot, o])
                for o, dst in ((0, gg_hbm), (1, ug_hbm))
            ]

        def body(i, carry):
            slot = lax.rem(i, 2)

            @pl.when(i >= 2)
            def _():
                for copy in tile(i - 2, slot):
                    copy.wait()

            cols = pl.ds(pl.multiple_of(i * bw, 128), bw)
            x = rows[X, :, :, :, cols].reshape(CHUNKS * chunk_rows, bw)
            out = dot(x, grads[...], TN).astype(BF16)
            stage(slot, 0)[...] = out[:, :quarter]
            stage(slot, 1)[...] = out[:, quarter:]
            for copy in tile(i, slot):
                copy.start()
            return carry

        n = width // bw
        lax.fori_loop(0, n, body, 0)
        for i in (n - 2, n - 1):
            for copy in tile(i, i % 2):
                copy.wait()

    def fill_out(a, c):
        fill(a, c)
        dispatch(a, c)

    for copy in loads[:OCT]:
        copy.wait()
    for c in range(CHUNKS):
        build_q(c)
        fill(X, c)
        if c < 2:
            dispatch(X, c)
    for copy in loads[OCT:]:
        copy.start()
    for copy in swaps[:first_cotangent]:
        copy.wait_recv()
    partner_keys = tuple(slot_keys(ids_in[i])[0] for i in range(2))
    for c in range(2):
        build_q(c, partner_keys)
        fill_out(V, c)
    for copy in loads[OCT:]:
        copy.wait()
    for j in range(OCT):
        tok[SOURCE[Y], j] = (tok[SOURCE[Y], j].astype(F32) * probs).astype(BF16)
    build_q(0)
    fill_out(Y, 0)
    for copy in swaps[first_cotangent:]:
        copy.wait_recv()
    for j in range(OCT):
        scale = upright(probs_in[j // (OCT // 2)])
        tok[SOURCE[Z], j] = (tok[SOURCE[Z], j].astype(F32) * scale).astype(BF16)
    build_q(0, partner_keys)
    fill_out(Z, 0)
    dispatch(X, 2)
    build_q(2, partner_keys)
    fill_out(V, 2)
    build_q(1)
    fill_out(Y, 1)
    own(0)
    own(1)
    lent(0)
    lent(1)
    for c in range(2):
        dispatched(V, c).wait_send()
    build_q(1, partner_keys)
    fill_out(Z, 1)
    build_q(2)
    fill_out(Y, 2)
    for copy in weights:
        copy.wait()
    collect(Y, 0)
    collect(Z, 0)
    partial(0)
    own(2)
    complete(0)
    forward(0)
    lent(2)
    dispatched(V, 2).wait_send()
    build_q(2, partner_keys)
    fill_out(Z, 2)
    backward(0)
    start_reduce(0)
    collect(Y, 1)
    complete(1)
    forward(1)
    collect(Z, 1)
    partial(1)
    pass_on(0)
    backward(1)
    start_reduce(1)
    complete(2)
    forward(2)
    collect(Y, 2)
    collect(Z, 2)
    partial(2)
    finish(0)
    pass_on(1)
    backward(2)
    start_reduce(2)
    finish(1)
    pass_on(2)
    weight_grads()
    finish(2)
    for c in range(CHUNKS):
        sent(c)
        for a in (Y, Z):
            dispatched(a, c).wait_send()
        for i in range(2):
            exchange(c, i).wait_send()
        for p in range(2):
            for way in range(2):
                for slot in range(3):
                    toward(c, p, way, slot).wait_send()
        pltpu.make_async_copy(send.at[X, c, me_e], back.at[c, me_e], retown_sem.at[c]).wait()
        scattered(send.at[X, c], back.at[c], ret_send.at[c], ret_recv.at[c]).wait()
    for i in range(2):
        swap_weight(i).wait_send()
    for copy in swaps:
        copy.wait_send()


def place(ids_ref, back_hbm, gg_src, ug_src, tg_hbm, gg_hbm, ug_hbm, back, rows, out, grad, back_sem, tg_sem, in_sem, out_sem):
    width = gg_src.shape[0]
    n_e = back.shape[1]
    oct_w = back.shape[3]
    cut = width // (OCT // 2)
    came = [pltpu.make_async_copy(back_hbm.at[c], back.at[c], back_sem.at[c]) for c in range(CHUNKS)]
    moves = []
    for j in range(OCT):
        o, at = j % 2, pl.ds((j // 2) * cut, cut)
        src, dst = ((gg_src, gg_hbm), (ug_src, ug_hbm))[o]
        moves.append(
            (
                pltpu.make_async_copy(src.at[at], grad.at[o, at], in_sem.at[j]),
                pltpu.make_async_copy(grad.at[o, at], dst.at[at], out_sem.at[j]),
            )
        )
    for copy in came:
        copy.start()
    for copy, _ in moves:
        copy.start()
    _, (rank_col, key_col) = slot_keys(ids_ref[...])
    half = n_e // 2 * SLAB
    per_half = n_e // 2 * PER
    slot, col = iota((half, half), 0), iota((half, half), 1)
    j, rest = slot // per_half, slot % per_half
    order = jnp.where(col == (rest // PER) * SLAB + j * PER + rest % PER, 1.0, 0.0).astype(BF16)
    at = (rank_col // PER) * (n_e * PER) + key_col
    here = jnp.where(at == iota((1, CHUNKS * n_e * PER), 1), 1.0, 0.0).astype(BF16)
    for c in range(CHUNKS):
        came[c].wait()
        for h in range(2):
            block = back[c, h * (n_e // 2) : (h + 1) * (n_e // 2)].reshape(half, oct_w)
            flat = dot(order, block).astype(BF16)
            first = c * n_e * PER + h * per_half
            for j in range(OCT):
                rows[first : first + per_half, j * oct_w : (j + 1) * oct_w] = flat[
                    j * per_half : (j + 1) * per_half
                ]
    outs = []
    for j in range(OCT):
        out[j] = dot(here, rows[:, j * oct_w : (j + 1) * oct_w]).astype(BF16)
        outs.append(
            pltpu.make_async_copy(out.at[j], tg_hbm.at[:, pl.ds(j * oct_w, oct_w)], tg_sem.at[j])
        )
        outs[-1].start()
        moves[j][0].wait()
        moves[j][1].start()
    for copy in outs:
        copy.wait()
    for _, copy in moves:
        copy.wait()


def local(tokens, out_grad, expert_ids, route_probs, w_gate, w_up, w_down):
    n_e = lax.axis_size("expert")
    n_x = lax.axis_size("dp")
    toks, width = tokens.shape
    gate_w, up_w, down_w = w_gate[0], w_up[0], w_down[0]
    quarter = gate_w.shape[1]
    oct_w = width // OCT
    chunk_rows = n_x * n_e * PER
    bw = 512 if width % 512 == 0 else 128
    vmem = pl.BlockSpec(memory_space=pltpu.VMEM)
    hbm = pl.BlockSpec(memory_space=pl.ANY)
    dma = pltpu.SemaphoreType.DMA
    ids_row = expert_ids.reshape(1, toks)
    back, gate_grad, up_grad, _, _ = pl.pallas_call(
        kernel,
        out_shape=(
            jax.ShapeDtypeStruct((CHUNKS, n_e, SLAB, oct_w), BF16),
            jax.ShapeDtypeStruct((width, quarter), BF16),
            jax.ShapeDtypeStruct((width, quarter), BF16),
            jax.ShapeDtypeStruct((CHUNKS - 1, 2, 2, n_e, width), BF16),
            jax.ShapeDtypeStruct((4, CHUNKS, n_e, SLAB, oct_w), BF16),
        ),
        in_specs=[vmem] * 2 + [hbm] * 5,
        out_specs=(hbm,) * 5,
        scratch_shapes=[
            pltpu.VMEM((3, OCT, toks, oct_w), BF16),
            pltpu.VMEM((max(n_e * SLAB, bw), max(OCT * toks, 4 * quarter)), BF16),
            pltpu.VMEM((width, quarter), BF16),
            pltpu.VMEM((width, quarter), BF16),
            pltpu.VMEM((quarter, width), BF16),
            pltpu.VMEM((2, quarter, width // 2), BF16),
            pltpu.VMEM((3, CHUNKS, n_e, SLAB, oct_w), BF16),
            pltpu.VMEM((n_e, SLAB, oct_w), BF16),
            pltpu.VMEM((2, 1, toks), jnp.int32),
            pltpu.VMEM((2, 1, toks), F32),
            pltpu.VMEM((2, CHUNKS, 2 * n_x, n_e, width), BF16),
            pltpu.VMEM((CHUNKS, 2, n_e, width), BF16),
            pltpu.VMEM((2, 2, n_e, width), BF16),
            pltpu.VMEM((3, n_x, n_e * PER, quarter), F32),
            pltpu.VMEM((2, 2 * n_e * PER, quarter), F32),
            pltpu.VMEM((CHUNKS, 2, 2 * n_e * PER, quarter), BF16),
            pltpu.VMEM((CHUNKS, 2, 2 * n_e * PER, quarter), BF16),
            pltpu.VMEM((CHUNKS * chunk_rows, 2 * quarter), BF16),
            dma((3, OCT)),
            dma((4, CHUNKS)),
            dma((4, CHUNKS)),
            dma((4, CHUNKS)),
            dma((CHUNKS, 2, 2)),
            dma((CHUNKS, 2, 2)),
            dma((2, OCT)),
            dma((2, OCT)),
            dma((2, 2)),
            dma((2, 2)),
            dma((2,)),
            dma((2,)),
            dma((CHUNKS, 2)),
            dma((CHUNKS, 2)),
            dma((CHUNKS, 2, 2, 3)),
            dma((CHUNKS, 2, 2, 3)),
            dma((CHUNKS,)),
            dma((CHUNKS,)),
            dma((CHUNKS,)),
            dma((2, 2)),
            dma((2,)),
        ],
        compiler_params=pltpu.CompilerParams(
            collective_id=0, has_side_effects=True, vmem_limit_bytes=127 * 2**19
        ),
    )(
        ids_row,
        route_probs.reshape(1, toks),
        tokens,
        out_grad,
        gate_w,
        up_w,
        down_w,
    )
    token_grad, gate_grad, up_grad = pl.pallas_call(
        place,
        out_shape=(
            jax.ShapeDtypeStruct((toks, width), BF16),
            jax.ShapeDtypeStruct((width, quarter), BF16),
            jax.ShapeDtypeStruct((width, quarter), BF16),
        ),
        in_specs=[vmem] + [hbm] * 3,
        out_specs=(hbm, hbm, hbm),
        scratch_shapes=[
            pltpu.VMEM((CHUNKS, n_e, SLAB, oct_w), BF16),
            pltpu.VMEM((CHUNKS * n_e * PER, width), BF16),
            pltpu.VMEM((OCT, toks, oct_w), BF16),
            pltpu.VMEM((2, width, quarter), BF16),
            dma((CHUNKS,)),
            dma((OCT,)),
            dma((OCT,)),
            dma((OCT,)),
        ],
        compiler_params=pltpu.CompilerParams(vmem_limit_bytes=60 * 2**20),
    )(ids_row, back, gate_grad, up_grad)
    return token_grad, gate_grad[None], up_grad[None]


def solution(mesh):
    in_specs = (
        P(("dp", "expert"), None),
        P(("dp", "expert"), None),
        P(("dp", "expert"), None),
        P(("dp", "expert"), None),
        P("expert", None, "dp"),
        P("expert", None, "dp"),
        P("expert", "dp", None),
    )
    out_specs = (P(("dp", "expert"), None), P("expert", None, "dp"), P("expert", None, "dp"))
    return jax.shard_map(local, mesh=mesh, in_specs=in_specs, out_specs=out_specs, check_vma=False)
```

```python
import jax
import jax.numpy as jnp
from jax import lax
from jax.experimental import pallas as pl
from jax.experimental.pallas import tpu as pltpu
from jax.sharding import PartitionSpec as P

MESH = pl.DeviceIdType.MESH
F32, BF16 = jnp.float32, jnp.bfloat16
CHUNKS = 3
PER = 2
OCT = 8
SLAB = PER * OCT
X, Y, Z, V = 0, 1, 2, 3
SOURCE = (0, 0, 1, 2)
NN = (((1,), (0,)), ((), ()))
NT = (((1,), (1,)), ((), ()))
TN = (((0,), (0,)), ((), ()))


def dot(a, b, dims=NN):
    return lax.dot_general(a, b, dims, preferred_element_type=F32)


def iota(shape, axis):
    return lax.broadcasted_iota(jnp.int32, shape, axis)


def slot_keys(ids_row):
    toks = ids_row.shape[1]
    first, second = iota((toks, toks), 0), iota((toks, toks), 1)
    ids_col = upright(ids_row)
    same = ids_col == ids_row
    rank_row = jnp.sum(jnp.where(same & (first < second), 1, 0), axis=0, keepdims=True)
    rank_col = jnp.sum(jnp.where(same & (second < first), 1, 0), axis=1, keepdims=True)
    return (
        (rank_row, ids_row * PER + (rank_row & 1)),
        (rank_col, ids_col * PER + (rank_col & 1)),
    )


def upright(row):
    toks = row.shape[1]
    eye = iota((toks, toks), 0) == iota((toks, toks), 1)
    return jnp.sum(jnp.where(eye, row, jnp.zeros_like(row)), axis=1, keepdims=True)


def kernel(
    ids_ref, probs_ref, tok_hbm, og_hbm, wg_hbm, wu_hbm, wd_hbm,
    back, gg_hbm, ug_hbm, fin_hbm, recv,
    tok, q, wg, wu, wd, wp, send, slabs, ids_in, probs_in, rows, relay, fin, acc, part_acc, ex_out, ex_in, grads,
    load_sem, disp_send, disp_recv, own_sem, ag_send, ag_recv, raw_send, raw_recv, meta_send, meta_recv, w_send, w_recv,
    ex_send, ex_recv, rs_send, rs_recv, ret_send, ret_recv, retown_sem, out_sem, fin_sem,
):
    n_x = lax.axis_size("dp")
    n_e = lax.axis_size("expert")
    me_x = lax.axis_index("dp")
    me_e = lax.axis_index("expert")
    nbr = (lax.rem(me_x + 1, n_x), lax.rem(me_x + n_x - 1, n_x))
    far = lax.rem(me_x + 2, n_x)
    pair = (me_x + 1 - 2 * lax.rem(me_x, 2), n_x - 1 - me_x)
    toks, width = tok_hbm.shape
    oct_w = width // OCT
    quarter = wg_hbm.shape[1]
    half = n_e
    gs = n_e // 2
    chunk_rows = n_x * n_e * PER
    log_half = half.bit_length() - 1

    barrier = pltpu.get_barrier_semaphore()

    def greet(d, carry):
        pl.semaphore_signal(
            barrier, inc=1, device_id=(me_x, lax.rem(me_e + d, n_e)), device_id_type=MESH
        )
        return carry

    lax.fori_loop(1, n_e, greet, 0)
    for x in nbr:
        pl.semaphore_signal(barrier, inc=1, device_id=(x, me_e), device_id_type=MESH)

    loads = [
        pltpu.make_async_copy(
            src.at[:, pl.ds(j * oct_w, oct_w)], tok.at[SOURCE[a], j], load_sem.at[a, j]
        )
        for a, src in ((X, tok_hbm), (Y, og_hbm))
        for j in range(OCT)
    ]
    for copy in loads[:OCT]:
        copy.start()
    weights = [
        pltpu.make_async_copy(src, dst, load_sem.at[2, i])
        for i, (src, dst) in enumerate(((wg_hbm, wg), (wu_hbm, wu), (wd_hbm, wd)))
    ]
    for w in weights:
        w.start()

    wide = width // 2

    def swap_weight(i):
        return pltpu.make_async_remote_copy(
            src_ref=wd_hbm.at[:, pl.ds(i * wide, wide)],
            dst_ref=wp.at[i],
            send_sem=w_send.at[i],
            recv_sem=w_recv.at[i],
            device_id=(pair[i], me_e),
            device_id_type=MESH,
        )

    def swap(src, dst, i, send_sem, recv_sem):
        return pltpu.make_async_remote_copy(
            src_ref=src,
            dst_ref=dst,
            send_sem=send_sem,
            recv_sem=recv_sem,
            device_id=(pair[1 - i], me_e),
            device_id_type=MESH,
        )

    swaps = []
    for i in range(2):
        for n, (src, dst) in enumerate(((ids_ref, ids_in), (probs_ref, probs_in))):
            swaps.append(swap(src, dst.at[i], i, meta_send.at[i, n], meta_recv.at[i, n]))
    for a, whole in ((V, tok_hbm), (Z, og_hbm)):
        for j in range(OCT // 2):
            for i in range(2):
                at = i * (OCT // 2) + j
                src = whole.at[:, pl.ds(at * oct_w, oct_w)]
                n = a - Z
                dst = tok.at[SOURCE[a], at]
                swaps.append(swap(src, dst, i, raw_send.at[n, at], raw_recv.at[n, at]))
    first_cotangent = len(swaps) - OCT

    pl.semaphore_wait(barrier, n_e - 1 + 2)
    for copy in swaps:
        copy.start()
    for i in range(2):
        swap_weight(i).start()

    (rank_row, key_row), _ = slot_keys(ids_ref[...])
    probs = upright(probs_ref[...])

    n_slab_rows = n_e * SLAB
    step = min(256, n_slab_rows)

    def build_q(c, keys=((rank_row, key_row),) * 2):
        for part, (rank, key) in enumerate(keys):

            def body(j, carry):
                keyc = jnp.where((rank >> 1) == c, key, -1)
                i = iota((n_slab_rows, 1), 0)
                want = jnp.where(((i >> 1) & (OCT - 1)) == j, (i >> 4) * PER + (i & 1), -2)
                cols = pl.ds(pl.multiple_of(j * toks, toks), toks)
                q[:n_slab_rows, cols] = jnp.where(want == keyc, 1.0, 0.0).astype(BF16)
                return carry

            lax.fori_loop(part * (OCT // 2), (part + 1) * (OCT // 2), body, 0)

    def slab_of(a, c):
        return send.at[((Y, 2), (Z, 1), (Z, 2))[c] if a == V else (a, c)]

    def fill(a, c):
        def body(m, carry):
            part = q[pl.ds(pl.multiple_of(m * step, step), step), : OCT * toks]
            out = dot(part, tok[SOURCE[a]].reshape(OCT * toks, oct_w)).astype(BF16)
            slab_of(a, c)[pl.ds(m * (step // SLAB), step // SLAB)] = out.reshape(
                step // SLAB, SLAB, oct_w
            )
            return carry

        lax.fori_loop(0, n_slab_rows // step, body, 0)

    def scatter(src, dst, send_sem, recv_sem, self_sem):
        pltpu.make_async_copy(src.at[me_e], dst.at[me_e], self_sem).start()

        def body(d, carry):
            peer = lax.rem(me_e + d, n_e)
            pltpu.make_async_remote_copy(
                src_ref=src.at[peer],
                dst_ref=dst.at[me_e],
                send_sem=send_sem,
                recv_sem=recv_sem,
                device_id=(me_x, peer),
                device_id_type=MESH,
            ).start()
            return carry

        lax.fori_loop(1, n_e, body, 0)

    def scattered(src, dst, send_sem, recv_sem):
        return pltpu.make_async_remote_copy(
            src_ref=src.at[pl.ds(0, n_e - 1)],
            dst_ref=dst.at[pl.ds(0, n_e - 1)],
            send_sem=send_sem,
            recv_sem=recv_sem,
            device_id=(nbr[0], me_e),
            device_id_type=MESH,
        )

    def dispatch(a, c):
        scatter(
            slab_of(a, c), recv.at[a, c], disp_send.at[a, c], disp_recv.at[a, c], own_sem.at[a, c]
        )

    def dispatched(a, c):
        return scattered(slab_of(a, c), recv.at[a, c], disp_send.at[a, c], disp_recv.at[a, c])

    def share(c, i, n, block):
        ref = rows.at[X, c, pl.ds(block * 2, 2), :, pl.ds(i * wide, wide)]
        return pltpu.make_async_remote_copy(
            src_ref=ref,
            dst_ref=ref,
            send_sem=ag_send.at[c, i, n],
            recv_sem=ag_recv.at[c, i, n],
            device_id=(pair[i], me_e),
            device_id_type=MESH,
        )

    size = gs * SLAB
    piece = half // 2
    piece_size = size // 2

    def perm(row, col):
        j, rest = row >> log_half, row & (half - 1)
        at = rest >> 1
        slab = (at & (gs // 2 - 1)) * 2 + (at >> (log_half - 2))
        return jnp.where(col == slab * SLAB + j * PER + (rest & 1), 1.0, 0.0).astype(BF16)

    def piece_perm(row, col):
        j, rest = row >> (log_half - 1), row & (piece - 1)
        return jnp.where(col == (rest >> 1) * SLAB + j * PER + (rest & 1), 1.0, 0.0).astype(BF16)

    def collect(a, c):
        pltpu.make_async_copy(slab_of(a, c).at[me_e], recv.at[a, c, me_e], own_sem.at[a, c]).wait()
        dispatched(a, c).wait_recv()
        load = pltpu.make_async_copy(recv.at[a, c], slabs, own_sem.at[a, c])
        load.start()
        load.wait()
        order = perm(iota((size, size), 0), iota((size, size), 1))
        dst = X if a in (X, V) else Y
        block_at = {X: (me_x, me_x), Y: (me_x, me_x), Z: (far, far), V: (pair[1], pair[0])}[a]
        for h in range(2):
            block = slabs[h * gs : (h + 1) * gs].reshape(size, oct_w)
            out = dot(order, block).astype(BF16)
            for j in range(OCT):
                rows[
                    dst, c, block_at[j // (OCT // 2)] * 2 + h, :, j * oct_w : (j + 1) * oct_w
                ] = out[
                    j * half : (j + 1) * half
                ]

    def own(c):
        collect(X, c)
        for i in range(2):
            share(c, i, 0, me_x).start()

    def lent(c):
        collect(V, c)
        for i in range(2):
            share(c, i, 1, pair[1 - i]).start()

    def exchange(c, i):
        return pltpu.make_async_remote_copy(
            src_ref=ex_out.at[c, i],
            dst_ref=ex_in.at[c, i],
            send_sem=ex_send.at[c, i],
            recv_sem=ex_recv.at[c, i],
            device_id=(pair[i], me_e),
            device_id_type=MESH,
        )

    def complete(c):
        for i in range(2):
            share(c, i, 0, pair[i]).wait_recv()
            share(c, i, 1, far).wait_recv()

    def sent(c):
        for i in range(2):
            share(c, i, 0, me_x).wait_send()
            share(c, i, 1, pair[1 - i]).wait_send()

    kw = width // 4

    def forward(c):
        def body(k, carry):
            cols = pl.ds(pl.multiple_of(k * kw, 128), kw)
            x = rows[X, c, :, :, cols].reshape(chunk_rows, kw)
            g = dot(x, wg[cols, :]).reshape(acc.shape[1:])
            u = dot(x, wu[cols, :]).reshape(acc.shape[1:])

            @pl.when(k == 0)
            def _():
                acc[0] = g
                acc[1] = u

            @pl.when(k > 0)
            def _():
                acc[0] += g
                acc[1] += u

            return carry

        lax.fori_loop(0, 4, body, 0)

    bw = 512 if width % 512 == 0 else 128

    block_rows = 2 * half

    def partial(c):
        for i in range(2):
            if c == 0:
                swap_weight(i).wait_recv()

            def body(k, carry):
                step_w = wide // 4
                near = pl.ds(pl.multiple_of(k * step_w, 128), step_w)
                cols = pl.ds(pl.multiple_of(i * wide + k * step_w, 128), step_w)
                y = jnp.concatenate(
                    [
                        rows[Y, c, pl.ds(p * 2, 2), :, cols].reshape(block_rows, step_w)
                        for p in (me_x, far)
                    ],
                    axis=0,
                )
                mine = dot(y, wd[:, cols], NT)
                other = dot(y, wp[i, :, near], NT)

                @pl.when(k == 0)
                def _():
                    part_acc[0] = mine
                    part_acc[1] = other

                @pl.when(k > 0)
                def _():
                    part_acc[0] += mine
                    part_acc[1] += other

                return carry

            lax.fori_loop(0, 4, body, 0)
            ex_out[c, i] = part_acc[1].astype(BF16)
            exchange(c, i).start()
            if i == 0:
                acc[2, me_x] = part_acc[0, :block_rows]
            else:
                acc[2, me_x] += part_acc[0, :block_rows]
            acc[2, pair[1 - i]] = part_acc[0, block_rows:]

    def backward(c):
        for i in range(2):
            exchange(c, i).wait_recv()
        for i in range(2):
            acc[2, pair[i]] += ex_in[c, i, :block_rows].astype(F32)
        acc[2, far] = ex_in[c, 0, block_rows:].astype(F32) + ex_in[c, 1, block_rows:].astype(F32)
        gate_val, up_val, hidden = (acc[n].reshape(chunk_rows, quarter) for n in range(3))
        s = jax.nn.sigmoid(gate_val)
        grad_up = (hidden * gate_val * s).astype(BF16)
        grad_gate = (hidden * up_val * s * (1.0 + gate_val * (1.0 - s))).astype(BF16)
        grads[c * chunk_rows : (c + 1) * chunk_rows, :quarter] = grad_gate
        grads[c * chunk_rows : (c + 1) * chunk_rows, quarter:] = grad_up

        def part(d, carry):
            cols = pl.ds(pl.multiple_of(d * bw, 128), bw)
            g = grads[c * chunk_rows : (c + 1) * chunk_rows, :quarter]
            u = grads[c * chunk_rows : (c + 1) * chunk_rows, quarter:]
            out = dot(g, wg[cols, :], NT) + dot(u, wu[cols, :], NT)
            rows[Y, c, :, :, cols] = out.astype(BF16).reshape(2 * n_x, half, bw)
            return carry

        lax.fori_loop(0, width // bw, part, 0)

    def last_of(c):
        return fin if c == CHUNKS - 1 else fin_hbm.at[c]

    def toward(c, p, way, slot):
        dst_block = far if slot == 0 else nbr[way]
        h = (way, 1 - way, way)[slot]
        part = pl.ds(p * piece, piece)
        src = rows.at[Y, c, dst_block * 2 + h, part]
        dst = relay.at[c, way, part] if slot == 0 else last_of(c).at[way, h, part]
        return pltpu.make_async_remote_copy(
            src_ref=src,
            dst_ref=dst,
            send_sem=rs_send.at[c, p, way, slot],
            recv_sem=rs_recv.at[c, p, way, slot],
            device_id=(nbr[way], me_e),
            device_id_type=MESH,
        )

    def start_reduce(c):
        for p in range(2):
            for slot in range(2):
                for way in range(2):
                    toward(c, p, way, slot).start()

    def pass_on(c):
        for p in range(2):
            for way in range(2):
                toward(c, p, way, 0).wait_recv()

                def body(d, carry):
                    part = pl.ds(p * piece, piece)
                    cols = pl.ds(pl.multiple_of(d * bw, 128), bw)
                    at = nbr[way] * 2 + way
                    mine = rows[Y, c, at, part, cols].astype(F32)
                    total = mine + relay[c, way, part, cols].astype(F32)
                    rows[Y, c, at, part, cols] = total.astype(BF16)
                    return carry

                lax.fori_loop(0, width // bw, body, 0)
                toward(c, p, way, 2).start()

    def give_back(c, peer):
        pltpu.make_async_remote_copy(
            src_ref=send.at[X, c, peer],
            dst_ref=back.at[c, me_e],
            send_sem=ret_send.at[c],
            recv_sem=ret_recv.at[c],
            device_id=(me_x, peer),
            device_id_type=MESH,
        ).start()

    def finish(c):
        dispatched(X, c).wait_send()
        order = piece_perm(iota((piece_size, piece_size), 1), iota((piece_size, piece_size), 0))
        for p in range(2):
            part = slice(p * piece, (p + 1) * piece)
            for way in range(2):
                for slot in (1, 2):
                    toward(c, p, way, slot).wait_recv()
            for h in range(2):
                if c < CHUNKS - 1:
                    fetch = [
                        pltpu.make_async_copy(
                            fin_hbm.at[c, way, h, pl.ds(p * piece, piece)],
                            relay.at[c, way, pl.ds(p * piece, piece)],
                            fin_sem.at[way],
                        )
                        for way in range(2)
                    ]
                    for copy in fetch:
                        copy.start()
                    for copy in fetch:
                        copy.wait()
                    came = (relay.at[c, 0], relay.at[c, 1])
                else:
                    came = (fin.at[0, h], fin.at[1, h])
                blocks = []
                for j in range(OCT):
                    cols = slice(j * oct_w, (j + 1) * oct_w)
                    total = (
                        rows[Y, c, me_x * 2 + h, part, cols].astype(F32)
                        + came[0][part, cols].astype(F32)
                        + came[1][part, cols].astype(F32)
                    )
                    blocks.append(total.astype(BF16))
                out = dot(order, jnp.concatenate(blocks, axis=0)).astype(BF16)
                for i in range(gs // 2):
                    send[X, c, h * gs + 2 * i + p] = out[i * SLAB : (i + 1) * SLAB]

            def body(d, carry):
                give_back(c, lax.rem(me_e // 2 + d, n_e // 2) * 2 + p)
                return carry

            lax.fori_loop(1, n_e // 2, body, 0)

            @pl.when(lax.rem(me_e, 2) != p)
            def _():
                give_back(c, (me_e // 2) * 2 + p)

        pltpu.make_async_copy(send.at[X, c, me_e], back.at[c, me_e], retown_sem.at[c]).start()

    def stage(slot, o):
        return q.at[pl.ds(0, bw), pl.ds(pl.multiple_of((slot * 2 + o) * quarter, 128), quarter)]

    def weight_grads():
        def tile(i, slot):
            cols = pl.ds(pl.multiple_of(i * bw, 128), bw)
            return [
                pltpu.make_async_copy(stage(slot, o), dst.at[cols, :], out_sem.at[slot, o])
                for o, dst in ((0, gg_hbm), (1, ug_hbm))
            ]

        def body(i, carry):
            slot = lax.rem(i, 2)

            @pl.when(i >= 2)
            def _():
                for copy in tile(i - 2, slot):
                    copy.wait()

            cols = pl.ds(pl.multiple_of(i * bw, 128), bw)
            x = rows[X, :, :, :, cols].reshape(CHUNKS * chunk_rows, bw)
            out = dot(x, grads[...], TN).astype(BF16)
            stage(slot, 0)[...] = out[:, :quarter]
            stage(slot, 1)[...] = out[:, quarter:]
            for copy in tile(i, slot):
                copy.start()
            return carry

        n = width // bw
        lax.fori_loop(0, n, body, 0)
        for i in (n - 2, n - 1):
            for copy in tile(i, i % 2):
                copy.wait()

    def fill_out(a, c):
        fill(a, c)
        dispatch(a, c)

    for copy in loads[:OCT]:
        copy.wait()
    for c in range(CHUNKS):
        build_q(c)
        fill(X, c)
        if c < 2:
            dispatch(X, c)
    for copy in loads[OCT:]:
        copy.start()
    for copy in swaps[:first_cotangent]:
        copy.wait_recv()
    partner_keys = tuple(slot_keys(ids_in[i])[0] for i in range(2))
    for c in range(2):
        build_q(c, partner_keys)
        fill_out(V, c)
    for copy in loads[OCT:]:
        copy.wait()
    for j in range(OCT):
        tok[SOURCE[Y], j] = (tok[SOURCE[Y], j].astype(F32) * probs).astype(BF16)
    build_q(0)
    fill_out(Y, 0)
    for copy in swaps[first_cotangent:]:
        copy.wait_recv()
    for j in range(OCT):
        scale = upright(probs_in[j // (OCT // 2)])
        tok[SOURCE[Z], j] = (tok[SOURCE[Z], j].astype(F32) * scale).astype(BF16)
    build_q(0, partner_keys)
    fill_out(Z, 0)
    dispatch(X, 2)
    build_q(2, partner_keys)
    fill_out(V, 2)
    build_q(1)
    fill_out(Y, 1)
    own(0)
    own(1)
    lent(0)
    lent(1)
    for c in range(2):
        dispatched(V, c).wait_send()
    build_q(1, partner_keys)
    fill_out(Z, 1)
    build_q(2)
    fill_out(Y, 2)
    for copy in weights:
        copy.wait()
    collect(Y, 0)
    collect(Z, 0)
    partial(0)
    own(2)
    complete(0)
    forward(0)
    lent(2)
    dispatched(V, 2).wait_send()
    build_q(2, partner_keys)
    fill_out(Z, 2)
    backward(0)
    start_reduce(0)
    collect(Y, 1)
    complete(1)
    forward(1)
    collect(Z, 1)
    partial(1)
    pass_on(0)
    backward(1)
    start_reduce(1)
    complete(2)
    forward(2)
    collect(Y, 2)
    collect(Z, 2)
    partial(2)
    finish(0)
    pass_on(1)
    backward(2)
    start_reduce(2)
    finish(1)
    weight_grads()
    pass_on(2)
    finish(2)
    for c in range(CHUNKS):
        sent(c)
        for a in (Y, Z):
            dispatched(a, c).wait_send()
        for i in range(2):
            exchange(c, i).wait_send()
        for p in range(2):
            for way in range(2):
                for slot in range(3):
                    toward(c, p, way, slot).wait_send()
        pltpu.make_async_copy(send.at[X, c, me_e], back.at[c, me_e], retown_sem.at[c]).wait()
        scattered(send.at[X, c], back.at[c], ret_send.at[c], ret_recv.at[c]).wait()
    for i in range(2):
        swap_weight(i).wait_send()
    for copy in swaps:
        copy.wait_send()


def place(ids_ref, back_hbm, gg_src, ug_src, tg_hbm, gg_hbm, ug_hbm, back, rows, out, grad, back_sem, tg_sem, in_sem, out_sem):
    width = gg_src.shape[0]
    n_e = back.shape[1]
    oct_w = back.shape[3]
    cut = width // (OCT // 2)
    came = [pltpu.make_async_copy(back_hbm.at[c], back.at[c], back_sem.at[c]) for c in range(CHUNKS)]
    moves = []
    for j in range(OCT):
        o, at = j % 2, pl.ds((j // 2) * cut, cut)
        src, dst = ((gg_src, gg_hbm), (ug_src, ug_hbm))[o]
        moves.append(
            (
                pltpu.make_async_copy(src.at[at], grad.at[o, at], in_sem.at[j]),
                pltpu.make_async_copy(grad.at[o, at], dst.at[at], out_sem.at[j]),
            )
        )
    for copy in came:
        copy.start()
    for copy, _ in moves:
        copy.start()
    _, (rank_col, key_col) = slot_keys(ids_ref[...])
    half = n_e // 2 * SLAB
    per_half = n_e // 2 * PER
    slot, col = iota((half, half), 0), iota((half, half), 1)
    j, rest = slot // per_half, slot % per_half
    order = jnp.where(col == (rest // PER) * SLAB + j * PER + rest % PER, 1.0, 0.0).astype(BF16)
    at = (rank_col // PER) * (n_e * PER) + key_col
    here = jnp.where(at == iota((1, CHUNKS * n_e * PER), 1), 1.0, 0.0).astype(BF16)
    for c in range(CHUNKS):
        came[c].wait()
        for h in range(2):
            block = back[c, h * (n_e // 2) : (h + 1) * (n_e // 2)].reshape(half, oct_w)
            flat = dot(order, block).astype(BF16)
            first = c * n_e * PER + h * per_half
            for j in range(OCT):
                rows[first : first + per_half, j * oct_w : (j + 1) * oct_w] = flat[
                    j * per_half : (j + 1) * per_half
                ]
        for came_in, go_out in moves[(0, 2, 5)[c] : (2, 5, 8)[c]]:
            came_in.wait()
            go_out.start()
    outs = []
    for j in range(OCT):
        out[j] = dot(here, rows[:, j * oct_w : (j + 1) * oct_w]).astype(BF16)
        outs.append(
            pltpu.make_async_copy(out.at[j], tg_hbm.at[:, pl.ds(j * oct_w, oct_w)], tg_sem.at[j])
        )
        outs[-1].start()
    for copy in outs:
        copy.wait()
    for _, copy in moves:
        copy.wait()


def local(tokens, out_grad, expert_ids, route_probs, w_gate, w_up, w_down):
    n_e = lax.axis_size("expert")
    n_x = lax.axis_size("dp")
    toks, width = tokens.shape
    gate_w, up_w, down_w = w_gate[0], w_up[0], w_down[0]
    quarter = gate_w.shape[1]
    oct_w = width // OCT
    chunk_rows = n_x * n_e * PER
    bw = 512 if width % 512 == 0 else 128
    vmem = pl.BlockSpec(memory_space=pltpu.VMEM)
    hbm = pl.BlockSpec(memory_space=pl.ANY)
    dma = pltpu.SemaphoreType.DMA
    ids_row = expert_ids.reshape(1, toks)
    back, gate_grad, up_grad, _, _ = pl.pallas_call(
        kernel,
        out_shape=(
            jax.ShapeDtypeStruct((CHUNKS, n_e, SLAB, oct_w), BF16),
            jax.ShapeDtypeStruct((width, quarter), BF16),
            jax.ShapeDtypeStruct((width, quarter), BF16),
            jax.ShapeDtypeStruct((CHUNKS - 1, 2, 2, n_e, width), BF16),
            jax.ShapeDtypeStruct((4, CHUNKS, n_e, SLAB, oct_w), BF16),
        ),
        in_specs=[vmem] * 2 + [hbm] * 5,
        out_specs=(hbm,) * 5,
        scratch_shapes=[
            pltpu.VMEM((3, OCT, toks, oct_w), BF16),
            pltpu.VMEM((max(n_e * SLAB, bw), max(OCT * toks, 4 * quarter)), BF16),
            pltpu.VMEM((width, quarter), BF16),
            pltpu.VMEM((width, quarter), BF16),
            pltpu.VMEM((quarter, width), BF16),
            pltpu.VMEM((2, quarter, width // 2), BF16),
            pltpu.VMEM((3, CHUNKS, n_e, SLAB, oct_w), BF16),
            pltpu.VMEM((n_e, SLAB, oct_w), BF16),
            pltpu.VMEM((2, 1, toks), jnp.int32),
            pltpu.VMEM((2, 1, toks), F32),
            pltpu.VMEM((2, CHUNKS, 2 * n_x, n_e, width), BF16),
            pltpu.VMEM((CHUNKS, 2, n_e, width), BF16),
            pltpu.VMEM((2, 2, n_e, width), BF16),
            pltpu.VMEM((3, n_x, n_e * PER, quarter), F32),
            pltpu.VMEM((2, 2 * n_e * PER, quarter), F32),
            pltpu.VMEM((CHUNKS, 2, 2 * n_e * PER, quarter), BF16),
            pltpu.VMEM((CHUNKS, 2, 2 * n_e * PER, quarter), BF16),
            pltpu.VMEM((CHUNKS * chunk_rows, 2 * quarter), BF16),
            dma((3, OCT)),
            dma((4, CHUNKS)),
            dma((4, CHUNKS)),
            dma((4, CHUNKS)),
            dma((CHUNKS, 2, 2)),
            dma((CHUNKS, 2, 2)),
            dma((2, OCT)),
            dma((2, OCT)),
            dma((2, 2)),
            dma((2, 2)),
            dma((2,)),
            dma((2,)),
            dma((CHUNKS, 2)),
            dma((CHUNKS, 2)),
            dma((CHUNKS, 2, 2, 3)),
            dma((CHUNKS, 2, 2, 3)),
            dma((CHUNKS,)),
            dma((CHUNKS,)),
            dma((CHUNKS,)),
            dma((2, 2)),
            dma((2,)),
        ],
        compiler_params=pltpu.CompilerParams(
            collective_id=0, has_side_effects=True, vmem_limit_bytes=127 * 2**19
        ),
    )(
        ids_row,
        route_probs.reshape(1, toks),
        tokens,
        out_grad,
        gate_w,
        up_w,
        down_w,
    )
    token_grad, gate_grad, up_grad = pl.pallas_call(
        place,
        out_shape=(
            jax.ShapeDtypeStruct((toks, width), BF16),
            jax.ShapeDtypeStruct((width, quarter), BF16),
            jax.ShapeDtypeStruct((width, quarter), BF16),
        ),
        in_specs=[vmem] + [hbm] * 3,
        out_specs=(hbm, hbm, hbm),
        scratch_shapes=[
            pltpu.VMEM((CHUNKS, n_e, SLAB, oct_w), BF16),
            pltpu.VMEM((CHUNKS * n_e * PER, width), BF16),
            pltpu.VMEM((OCT, toks, oct_w), BF16),
            pltpu.VMEM((2, width, quarter), BF16),
            dma((CHUNKS,)),
            dma((OCT,)),
            dma((OCT,)),
            dma((OCT,)),
        ],
        compiler_params=pltpu.CompilerParams(vmem_limit_bytes=60 * 2**20),
    )(ids_row, back, gate_grad, up_grad)
    return token_grad, gate_grad[None], up_grad[None]


def solution(mesh):
    in_specs = (
        P(("dp", "expert"), None),
        P(("dp", "expert"), None),
        P(("dp", "expert"), None),
        P(("dp", "expert"), None),
        P("expert", None, "dp"),
        P("expert", None, "dp"),
        P("expert", "dp", None),
    )
    out_specs = (P(("dp", "expert"), None), P("expert", None, "dp"), P("expert", None, "dp"))
    return jax.shard_map(local, mesh=mesh, in_specs=in_specs, out_specs=out_specs, check_vma=False)
```

```python
import jax
import jax.numpy as jnp
from jax import lax
from jax.experimental import pallas as pl
from jax.experimental.pallas import tpu as pltpu
from jax.sharding import PartitionSpec as P

MESH = pl.DeviceIdType.MESH
F32, BF16 = jnp.float32, jnp.bfloat16
CHUNKS = 3
PER = 2
OCT = 8
SLAB = PER * OCT
X, Y, Z, V = 0, 1, 2, 3
SOURCE = (0, 0, 1, 2)
NN = (((1,), (0,)), ((), ()))
NT = (((1,), (1,)), ((), ()))
TN = (((0,), (0,)), ((), ()))


def dot(a, b, dims=NN):
    return lax.dot_general(a, b, dims, preferred_element_type=F32)


def iota(shape, axis):
    return lax.broadcasted_iota(jnp.int32, shape, axis)


def slot_keys(ids_row):
    toks = ids_row.shape[1]
    first, second = iota((toks, toks), 0), iota((toks, toks), 1)
    ids_col = upright(ids_row)
    same = ids_col == ids_row
    rank_row = jnp.sum(jnp.where(same & (first < second), 1, 0), axis=0, keepdims=True)
    rank_col = jnp.sum(jnp.where(same & (second < first), 1, 0), axis=1, keepdims=True)
    return (
        (rank_row, ids_row * PER + (rank_row & 1)),
        (rank_col, ids_col * PER + (rank_col & 1)),
    )


def upright(row):
    toks = row.shape[1]
    eye = iota((toks, toks), 0) == iota((toks, toks), 1)
    return jnp.sum(jnp.where(eye, row, jnp.zeros_like(row)), axis=1, keepdims=True)


def kernel(
    ids_ref, probs_ref, tok_hbm, og_hbm, wg_hbm, wu_hbm, wd_hbm,
    back, gg_hbm, ug_hbm, fin_hbm, recv,
    tok, q, wg, wu, wd, wp, send, slabs, ids_in, probs_in, rows, relay, fin, acc, part_acc, ex_out, ex_in, grads,
    load_sem, disp_send, disp_recv, own_sem, ag_send, ag_recv, raw_send, raw_recv, meta_send, meta_recv, w_send, w_recv,
    ex_send, ex_recv, rs_send, rs_recv, ret_send, ret_recv, retown_sem, out_sem, fin_sem,
):
    n_x = lax.axis_size("dp")
    n_e = lax.axis_size("expert")
    me_x = lax.axis_index("dp")
    me_e = lax.axis_index("expert")
    nbr = (lax.rem(me_x + 1, n_x), lax.rem(me_x + n_x - 1, n_x))
    far = lax.rem(me_x + 2, n_x)
    pair = (me_x + 1 - 2 * lax.rem(me_x, 2), n_x - 1 - me_x)
    toks, width = tok_hbm.shape
    oct_w = width // OCT
    quarter = wg_hbm.shape[1]
    half = n_e
    gs = n_e // 2
    chunk_rows = n_x * n_e * PER
    log_half = half.bit_length() - 1

    barrier = pltpu.get_barrier_semaphore()

    def greet(d, carry):
        pl.semaphore_signal(
            barrier, inc=1, device_id=(me_x, lax.rem(me_e + d, n_e)), device_id_type=MESH
        )
        return carry

    lax.fori_loop(1, n_e, greet, 0)
    for x in nbr:
        pl.semaphore_signal(barrier, inc=1, device_id=(x, me_e), device_id_type=MESH)

    loads = [
        pltpu.make_async_copy(
            src.at[:, pl.ds(j * oct_w, oct_w)], tok.at[SOURCE[a], j], load_sem.at[a, j]
        )
        for a, src in ((X, tok_hbm), (Y, og_hbm))
        for j in range(OCT)
    ]
    for copy in loads[:OCT]:
        copy.start()
    weights = [
        pltpu.make_async_copy(src, dst, load_sem.at[2, i])
        for i, (src, dst) in enumerate(((wg_hbm, wg), (wu_hbm, wu), (wd_hbm, wd)))
    ]
    for w in weights:
        w.start()

    wide = width // 2

    def swap_weight(i):
        return pltpu.make_async_remote_copy(
            src_ref=wd_hbm.at[:, pl.ds(i * wide, wide)],
            dst_ref=wp.at[i],
            send_sem=w_send.at[i],
            recv_sem=w_recv.at[i],
            device_id=(pair[i], me_e),
            device_id_type=MESH,
        )

    def swap(src, dst, i, send_sem, recv_sem):
        return pltpu.make_async_remote_copy(
            src_ref=src,
            dst_ref=dst,
            send_sem=send_sem,
            recv_sem=recv_sem,
            device_id=(pair[1 - i], me_e),
            device_id_type=MESH,
        )

    swaps = []
    for i in range(2):
        for n, (src, dst) in enumerate(((ids_ref, ids_in), (probs_ref, probs_in))):
            swaps.append(swap(src, dst.at[i], i, meta_send.at[i, n], meta_recv.at[i, n]))
    for a, whole in ((V, tok_hbm), (Z, og_hbm)):
        for j in range(OCT // 2):
            for i in range(2):
                at = i * (OCT // 2) + j
                src = whole.at[:, pl.ds(at * oct_w, oct_w)]
                n = a - Z
                dst = tok.at[SOURCE[a], at]
                swaps.append(swap(src, dst, i, raw_send.at[n, at], raw_recv.at[n, at]))
    first_cotangent = len(swaps) - OCT

    pl.semaphore_wait(barrier, n_e - 1 + 2)
    for copy in swaps:
        copy.start()
    for i in range(2):
        swap_weight(i).start()

    (rank_row, key_row), _ = slot_keys(ids_ref[...])
    probs = upright(probs_ref[...])

    n_slab_rows = n_e * SLAB
    step = min(256, n_slab_rows)

    def build_q(c, keys=((rank_row, key_row),) * 2):
        for part, (rank, key) in enumerate(keys):

            def body(j, carry):
                keyc = jnp.where((rank >> 1) == c, key, -1)
                i = iota((n_slab_rows, 1), 0)
                want = jnp.where(((i >> 1) & (OCT - 1)) == j, (i >> 4) * PER + (i & 1), -2)
                cols = pl.ds(pl.multiple_of(j * toks, toks), toks)
                q[:n_slab_rows, cols] = jnp.where(want == keyc, 1.0, 0.0).astype(BF16)
                return carry

            lax.fori_loop(part * (OCT // 2), (part + 1) * (OCT // 2), body, 0)

    def slab_of(a, c):
        return send.at[((Y, 2), (Z, 1), (Z, 2))[c] if a == V else (a, c)]

    def fill(a, c):
        def body(m, carry):
            part = q[pl.ds(pl.multiple_of(m * step, step), step), : OCT * toks]
            out = dot(part, tok[SOURCE[a]].reshape(OCT * toks, oct_w)).astype(BF16)
            slab_of(a, c)[pl.ds(m * (step // SLAB), step // SLAB)] = out.reshape(
                step // SLAB, SLAB, oct_w
            )
            return carry

        lax.fori_loop(0, n_slab_rows // step, body, 0)

    def scatter(src, dst, send_sem, recv_sem, self_sem):
        pltpu.make_async_copy(src.at[me_e], dst.at[me_e], self_sem).start()

        def body(d, carry):
            peer = lax.rem(me_e + d, n_e)
            pltpu.make_async_remote_copy(
                src_ref=src.at[peer],
                dst_ref=dst.at[me_e],
                send_sem=send_sem,
                recv_sem=recv_sem,
                device_id=(me_x, peer),
                device_id_type=MESH,
            ).start()
            return carry

        lax.fori_loop(1, n_e, body, 0)

    def scattered(src, dst, send_sem, recv_sem):
        return pltpu.make_async_remote_copy(
            src_ref=src.at[pl.ds(0, n_e - 1)],
            dst_ref=dst.at[pl.ds(0, n_e - 1)],
            send_sem=send_sem,
            recv_sem=recv_sem,
            device_id=(nbr[0], me_e),
            device_id_type=MESH,
        )

    def dispatch(a, c):
        scatter(
            slab_of(a, c), recv.at[a, c], disp_send.at[a, c], disp_recv.at[a, c], own_sem.at[a, c]
        )

    def dispatched(a, c):
        return scattered(slab_of(a, c), recv.at[a, c], disp_send.at[a, c], disp_recv.at[a, c])

    def share(c, i, n, block):
        ref = rows.at[X, c, pl.ds(block * 2, 2), :, pl.ds(i * wide, wide)]
        return pltpu.make_async_remote_copy(
            src_ref=ref,
            dst_ref=ref,
            send_sem=ag_send.at[c, i, n],
            recv_sem=ag_recv.at[c, i, n],
            device_id=(pair[i], me_e),
            device_id_type=MESH,
        )

    size = gs * SLAB
    piece = half // 2
    piece_size = size // 2

    def perm(row, col):
        j, rest = row >> log_half, row & (half - 1)
        at = rest >> 1
        slab = (at & (gs // 2 - 1)) * 2 + (at >> (log_half - 2))
        return jnp.where(col == slab * SLAB + j * PER + (rest & 1), 1.0, 0.0).astype(BF16)

    def piece_perm(row, col):
        j, rest = row >> (log_half - 1), row & (piece - 1)
        return jnp.where(col == (rest >> 1) * SLAB + j * PER + (rest & 1), 1.0, 0.0).astype(BF16)

    def collect(a, c):
        pltpu.make_async_copy(slab_of(a, c).at[me_e], recv.at[a, c, me_e], own_sem.at[a, c]).wait()
        dispatched(a, c).wait_recv()
        load = pltpu.make_async_copy(recv.at[a, c], slabs, own_sem.at[a, c])
        load.start()
        load.wait()
        order = perm(iota((size, size), 0), iota((size, size), 1))
        dst = X if a in (X, V) else Y
        block_at = {X: (me_x, me_x), Y: (me_x, me_x), Z: (far, far), V: (pair[1], pair[0])}[a]
        for h in range(2):
            block = slabs[h * gs : (h + 1) * gs].reshape(size, oct_w)
            out = dot(order, block).astype(BF16)
            for j in range(OCT):
                rows[
                    dst, c, block_at[j // (OCT // 2)] * 2 + h, :, j * oct_w : (j + 1) * oct_w
                ] = out[
                    j * half : (j + 1) * half
                ]

    def own(c):
        collect(X, c)
        for i in range(2):
            share(c, i, 0, me_x).start()

    def lent(c):
        collect(V, c)
        for i in range(2):
            share(c, i, 1, pair[1 - i]).start()

    def exchange(c, i):
        return pltpu.make_async_remote_copy(
            src_ref=ex_out.at[c, i],
            dst_ref=ex_in.at[c, i],
            send_sem=ex_send.at[c, i],
            recv_sem=ex_recv.at[c, i],
            device_id=(pair[i], me_e),
            device_id_type=MESH,
        )

    def complete(c):
        for i in range(2):
            share(c, i, 0, pair[i]).wait_recv()
            share(c, i, 1, far).wait_recv()

    def sent(c):
        for i in range(2):
            share(c, i, 0, me_x).wait_send()
            share(c, i, 1, pair[1 - i]).wait_send()

    kw = width // 4

    def forward(c):
        def body(k, carry):
            cols = pl.ds(pl.multiple_of(k * kw, 128), kw)
            x = rows[X, c, :, :, cols].reshape(chunk_rows, kw)
            g = dot(x, wg[cols, :]).reshape(acc.shape[1:])
            u = dot(x, wu[cols, :]).reshape(acc.shape[1:])

            @pl.when(k == 0)
            def _():
                acc[0] = g
                acc[1] = u

            @pl.when(k > 0)
            def _():
                acc[0] += g
                acc[1] += u

            return carry

        lax.fori_loop(0, 4, body, 0)

    bw = 512 if width % 512 == 0 else 128

    block_rows = 2 * half

    def partial(c):
        for i in range(2):
            if c == 0:
                swap_weight(i).wait_recv()

            def body(k, carry):
                step_w = wide // 4
                near = pl.ds(pl.multiple_of(k * step_w, 128), step_w)
                cols = pl.ds(pl.multiple_of(i * wide + k * step_w, 128), step_w)
                y = jnp.concatenate(
                    [
                        rows[Y, c, pl.ds(p * 2, 2), :, cols].reshape(block_rows, step_w)
                        for p in (me_x, far)
                    ],
                    axis=0,
                )
                mine = dot(y, wd[:, cols], NT)
                other = dot(y, wp[i, :, near], NT)

                @pl.when(k == 0)
                def _():
                    part_acc[0] = mine
                    part_acc[1] = other

                @pl.when(k > 0)
                def _():
                    part_acc[0] += mine
                    part_acc[1] += other

                return carry

            lax.fori_loop(0, 4, body, 0)
            ex_out[c, i] = part_acc[1].astype(BF16)
            exchange(c, i).start()
            if i == 0:
                acc[2, me_x] = part_acc[0, :block_rows]
            else:
                acc[2, me_x] += part_acc[0, :block_rows]
            acc[2, pair[1 - i]] = part_acc[0, block_rows:]

    def backward(c):
        for i in range(2):
            exchange(c, i).wait_recv()
        for i in range(2):
            acc[2, pair[i]] += ex_in[c, i, :block_rows].astype(F32)
        acc[2, far] = ex_in[c, 0, block_rows:].astype(F32) + ex_in[c, 1, block_rows:].astype(F32)
        gate_val, up_val, hidden = (acc[n].reshape(chunk_rows, quarter) for n in range(3))
        s = jax.nn.sigmoid(gate_val)
        grad_up = (hidden * gate_val * s).astype(BF16)
        grad_gate = (hidden * up_val * s * (1.0 + gate_val * (1.0 - s))).astype(BF16)
        grads[c * chunk_rows : (c + 1) * chunk_rows, :quarter] = grad_gate
        grads[c * chunk_rows : (c + 1) * chunk_rows, quarter:] = grad_up

        def part(d, carry):
            cols = pl.ds(pl.multiple_of(d * bw, 128), bw)
            g = grads[c * chunk_rows : (c + 1) * chunk_rows, :quarter]
            u = grads[c * chunk_rows : (c + 1) * chunk_rows, quarter:]
            out = dot(g, wg[cols, :], NT) + dot(u, wu[cols, :], NT)
            rows[Y, c, :, :, cols] = out.astype(BF16).reshape(2 * n_x, half, bw)
            return carry

        lax.fori_loop(0, width // bw, part, 0)

    def last_of(c):
        return fin if c == CHUNKS - 1 else fin_hbm.at[c]

    def toward(c, p, way, slot):
        dst_block = far if slot == 0 else nbr[way]
        h = (way, 1 - way, way)[slot]
        part = pl.ds(p * piece, piece)
        src = rows.at[Y, c, dst_block * 2 + h, part]
        dst = relay.at[c, way, part] if slot == 0 else last_of(c).at[way, h, part]
        return pltpu.make_async_remote_copy(
            src_ref=src,
            dst_ref=dst,
            send_sem=rs_send.at[c, p, way, slot],
            recv_sem=rs_recv.at[c, p, way, slot],
            device_id=(nbr[way], me_e),
            device_id_type=MESH,
        )

    def start_reduce(c):
        for p in range(2):
            for slot in range(2):
                for way in range(2):
                    toward(c, p, way, slot).start()

    def pass_on(c):
        for p in range(2):
            for way in range(2):
                toward(c, p, way, 0).wait_recv()

                def body(d, carry):
                    part = pl.ds(p * piece, piece)
                    cols = pl.ds(pl.multiple_of(d * bw, 128), bw)
                    at = nbr[way] * 2 + way
                    mine = rows[Y, c, at, part, cols].astype(F32)
                    total = mine + relay[c, way, part, cols].astype(F32)
                    rows[Y, c, at, part, cols] = total.astype(BF16)
                    return carry

                lax.fori_loop(0, width // bw, body, 0)
                toward(c, p, way, 2).start()

    def give_back(c, peer):
        pltpu.make_async_remote_copy(
            src_ref=send.at[X, c, peer],
            dst_ref=back.at[c, me_e],
            send_sem=ret_send.at[c],
            recv_sem=ret_recv.at[c],
            device_id=(me_x, peer),
            device_id_type=MESH,
        ).start()

    def finish(c):
        dispatched(X, c).wait_send()
        order = piece_perm(iota((piece_size, piece_size), 1), iota((piece_size, piece_size), 0))
        for p in range(2):
            part = slice(p * piece, (p + 1) * piece)
            for way in range(2):
                for slot in (1, 2):
                    toward(c, p, way, slot).wait_recv()
            for h in range(2):
                if c < CHUNKS - 1:
                    fetch = [
                        pltpu.make_async_copy(
                            fin_hbm.at[c, way, h, pl.ds(p * piece, piece)],
                            relay.at[c, way, pl.ds(p * piece, piece)],
                            fin_sem.at[way],
                        )
                        for way in range(2)
                    ]
                    for copy in fetch:
                        copy.start()
                    for copy in fetch:
                        copy.wait()
                    came = (relay.at[c, 0], relay.at[c, 1])
                else:
                    came = (fin.at[0, h], fin.at[1, h])
                blocks = []
                for j in range(OCT):
                    cols = slice(j * oct_w, (j + 1) * oct_w)
                    total = (
                        rows[Y, c, me_x * 2 + h, part, cols].astype(F32)
                        + came[0][part, cols].astype(F32)
                        + came[1][part, cols].astype(F32)
                    )
                    blocks.append(total.astype(BF16))
                out = dot(order, jnp.concatenate(blocks, axis=0)).astype(BF16)
                for i in range(gs // 2):
                    send[X, c, h * gs + 2 * i + p] = out[i * SLAB : (i + 1) * SLAB]

                def body(d, carry):
                    peer = h * gs + lax.rem(me_e // 2 + d, gs // 2) * 2 + p

                    @pl.when(peer != me_e)
                    def _():
                        give_back(c, peer)

                    return carry

                lax.fori_loop(0, gs // 2, body, 0)

        pltpu.make_async_copy(send.at[X, c, me_e], back.at[c, me_e], retown_sem.at[c]).start()

    def stage(slot, o):
        return q.at[pl.ds(0, bw), pl.ds(pl.multiple_of((slot * 2 + o) * quarter, 128), quarter)]

    def weight_grads():
        def tile(i, slot):
            cols = pl.ds(pl.multiple_of(i * bw, 128), bw)
            return [
                pltpu.make_async_copy(stage(slot, o), dst.at[cols, :], out_sem.at[slot, o])
                for o, dst in ((0, gg_hbm), (1, ug_hbm))
            ]

        def body(i, carry):
            slot = lax.rem(i, 2)

            @pl.when(i >= 2)
            def _():
                for copy in tile(i - 2, slot):
                    copy.wait()

            cols = pl.ds(pl.multiple_of(i * bw, 128), bw)
            x = rows[X, :, :, :, cols].reshape(CHUNKS * chunk_rows, bw)
            out = dot(x, grads[...], TN).astype(BF16)
            stage(slot, 0)[...] = out[:, :quarter]
            stage(slot, 1)[...] = out[:, quarter:]
            for copy in tile(i, slot):
                copy.start()
            return carry

        n = width // bw
        lax.fori_loop(0, n, body, 0)
        for i in (n - 2, n - 1):
            for copy in tile(i, i % 2):
                copy.wait()

    def fill_out(a, c):
        fill(a, c)
        dispatch(a, c)

    for copy in loads[:OCT]:
        copy.wait()
    for c in range(CHUNKS):
        build_q(c)
        fill(X, c)
        if c < 2:
            dispatch(X, c)
    for copy in loads[OCT:]:
        copy.start()
    for copy in swaps[:first_cotangent]:
        copy.wait_recv()
    partner_keys = tuple(slot_keys(ids_in[i])[0] for i in range(2))
    for c in range(2):
        build_q(c, partner_keys)
        fill_out(V, c)
    for copy in loads[OCT:]:
        copy.wait()
    for j in range(OCT):
        tok[SOURCE[Y], j] = (tok[SOURCE[Y], j].astype(F32) * probs).astype(BF16)
    build_q(0)
    fill_out(Y, 0)
    for copy in swaps[first_cotangent:]:
        copy.wait_recv()
    for j in range(OCT):
        scale = upright(probs_in[j // (OCT // 2)])
        tok[SOURCE[Z], j] = (tok[SOURCE[Z], j].astype(F32) * scale).astype(BF16)
    build_q(0, partner_keys)
    fill_out(Z, 0)
    dispatch(X, 2)
    build_q(2, partner_keys)
    fill_out(V, 2)
    build_q(1)
    fill_out(Y, 1)
    own(0)
    own(1)
    lent(0)
    lent(1)
    for c in range(2):
        dispatched(V, c).wait_send()
    build_q(1, partner_keys)
    fill_out(Z, 1)
    build_q(2)
    fill_out(Y, 2)
    for copy in weights:
        copy.wait()
    collect(Y, 0)
    collect(Z, 0)
    partial(0)
    own(2)
    complete(0)
    forward(0)
    lent(2)
    dispatched(V, 2).wait_send()
    build_q(2, partner_keys)
    fill_out(Z, 2)
    backward(0)
    start_reduce(0)
    collect(Y, 1)
    complete(1)
    forward(1)
    collect(Z, 1)
    partial(1)
    pass_on(0)
    backward(1)
    start_reduce(1)
    complete(2)
    forward(2)
    collect(Y, 2)
    collect(Z, 2)
    partial(2)
    finish(0)
    pass_on(1)
    backward(2)
    start_reduce(2)
    finish(1)
    weight_grads()
    pass_on(2)
    finish(2)
    for c in range(CHUNKS):
        sent(c)
        for a in (Y, Z):
            dispatched(a, c).wait_send()
        for i in range(2):
            exchange(c, i).wait_send()
        for p in range(2):
            for way in range(2):
                for slot in range(3):
                    toward(c, p, way, slot).wait_send()
        pltpu.make_async_copy(send.at[X, c, me_e], back.at[c, me_e], retown_sem.at[c]).wait()
        scattered(send.at[X, c], back.at[c], ret_send.at[c], ret_recv.at[c]).wait()
    for i in range(2):
        swap_weight(i).wait_send()
    for copy in swaps:
        copy.wait_send()


def place(ids_ref, back_hbm, gg_src, ug_src, tg_hbm, gg_hbm, ug_hbm, back, rows, out, grad, back_sem, tg_sem, in_sem, out_sem):
    width = gg_src.shape[0]
    n_e = back.shape[1]
    oct_w = back.shape[3]
    cut = width // (OCT // 2)
    came = [pltpu.make_async_copy(back_hbm.at[c], back.at[c], back_sem.at[c]) for c in range(CHUNKS)]
    moves = []
    for j in range(OCT):
        o, at = j % 2, pl.ds((j // 2) * cut, cut)
        src, dst = ((gg_src, gg_hbm), (ug_src, ug_hbm))[o]
        moves.append(
            (
                pltpu.make_async_copy(src.at[at], grad.at[o, at], in_sem.at[j]),
                pltpu.make_async_copy(grad.at[o, at], dst.at[at], out_sem.at[j]),
            )
        )
    for copy in came:
        copy.start()
    for copy, _ in moves:
        copy.start()
    _, (rank_col, key_col) = slot_keys(ids_ref[...])
    half = n_e // 2 * SLAB
    per_half = n_e // 2 * PER
    slot, col = iota((half, half), 0), iota((half, half), 1)
    j, rest = slot // per_half, slot % per_half
    order = jnp.where(col == (rest // PER) * SLAB + j * PER + rest % PER, 1.0, 0.0).astype(BF16)
    at = (rank_col // PER) * (n_e * PER) + key_col
    here = jnp.where(at == iota((1, CHUNKS * n_e * PER), 1), 1.0, 0.0).astype(BF16)
    for c in range(CHUNKS):
        came[c].wait()
        for h in range(2):
            block = back[c, h * (n_e // 2) : (h + 1) * (n_e // 2)].reshape(half, oct_w)
            flat = dot(order, block).astype(BF16)
            first = c * n_e * PER + h * per_half
            for j in range(OCT):
                rows[first : first + per_half, j * oct_w : (j + 1) * oct_w] = flat[
                    j * per_half : (j + 1) * per_half
                ]
        for came_in, go_out in moves[(0, 2, 5)[c] : (2, 5, 8)[c]]:
            came_in.wait()
            go_out.start()
    outs = []
    for j in range(OCT):
        out[j] = dot(here, rows[:, j * oct_w : (j + 1) * oct_w]).astype(BF16)
        outs.append(
            pltpu.make_async_copy(out.at[j], tg_hbm.at[:, pl.ds(j * oct_w, oct_w)], tg_sem.at[j])
        )
        outs[-1].start()
    for copy in outs:
        copy.wait()
    for _, copy in moves:
        copy.wait()


def local(tokens, out_grad, expert_ids, route_probs, w_gate, w_up, w_down):
    n_e = lax.axis_size("expert")
    n_x = lax.axis_size("dp")
    toks, width = tokens.shape
    gate_w, up_w, down_w = w_gate[0], w_up[0], w_down[0]
    quarter = gate_w.shape[1]
    oct_w = width // OCT
    chunk_rows = n_x * n_e * PER
    bw = 512 if width % 512 == 0 else 128
    vmem = pl.BlockSpec(memory_space=pltpu.VMEM)
    hbm = pl.BlockSpec(memory_space=pl.ANY)
    dma = pltpu.SemaphoreType.DMA
    ids_row = expert_ids.reshape(1, toks)
    back, gate_grad, up_grad, _, _ = pl.pallas_call(
        kernel,
        out_shape=(
            jax.ShapeDtypeStruct((CHUNKS, n_e, SLAB, oct_w), BF16),
            jax.ShapeDtypeStruct((width, quarter), BF16),
            jax.ShapeDtypeStruct((width, quarter), BF16),
            jax.ShapeDtypeStruct((CHUNKS - 1, 2, 2, n_e, width), BF16),
            jax.ShapeDtypeStruct((4, CHUNKS, n_e, SLAB, oct_w), BF16),
        ),
        in_specs=[vmem] * 2 + [hbm] * 5,
        out_specs=(hbm,) * 5,
        scratch_shapes=[
            pltpu.VMEM((3, OCT, toks, oct_w), BF16),
            pltpu.VMEM((max(n_e * SLAB, bw), max(OCT * toks, 4 * quarter)), BF16),
            pltpu.VMEM((width, quarter), BF16),
            pltpu.VMEM((width, quarter), BF16),
            pltpu.VMEM((quarter, width), BF16),
            pltpu.VMEM((2, quarter, width // 2), BF16),
            pltpu.VMEM((3, CHUNKS, n_e, SLAB, oct_w), BF16),
            pltpu.VMEM((n_e, SLAB, oct_w), BF16),
            pltpu.VMEM((2, 1, toks), jnp.int32),
            pltpu.VMEM((2, 1, toks), F32),
            pltpu.VMEM((2, CHUNKS, 2 * n_x, n_e, width), BF16),
            pltpu.VMEM((CHUNKS, 2, n_e, width), BF16),
            pltpu.VMEM((2, 2, n_e, width), BF16),
            pltpu.VMEM((3, n_x, n_e * PER, quarter), F32),
            pltpu.VMEM((2, 2 * n_e * PER, quarter), F32),
            pltpu.VMEM((CHUNKS, 2, 2 * n_e * PER, quarter), BF16),
            pltpu.VMEM((CHUNKS, 2, 2 * n_e * PER, quarter), BF16),
            pltpu.VMEM((CHUNKS * chunk_rows, 2 * quarter), BF16),
            dma((3, OCT)),
            dma((4, CHUNKS)),
            dma((4, CHUNKS)),
            dma((4, CHUNKS)),
            dma((CHUNKS, 2, 2)),
            dma((CHUNKS, 2, 2)),
            dma((2, OCT)),
            dma((2, OCT)),
            dma((2, 2)),
            dma((2, 2)),
            dma((2,)),
            dma((2,)),
            dma((CHUNKS, 2)),
            dma((CHUNKS, 2)),
            dma((CHUNKS, 2, 2, 3)),
            dma((CHUNKS, 2, 2, 3)),
            dma((CHUNKS,)),
            dma((CHUNKS,)),
            dma((CHUNKS,)),
            dma((2, 2)),
            dma((2,)),
        ],
        compiler_params=pltpu.CompilerParams(
            collective_id=0, has_side_effects=True, vmem_limit_bytes=127 * 2**19
        ),
    )(
        ids_row,
        route_probs.reshape(1, toks),
        tokens,
        out_grad,
        gate_w,
        up_w,
        down_w,
    )
    token_grad, gate_grad, up_grad = pl.pallas_call(
        place,
        out_shape=(
            jax.ShapeDtypeStruct((toks, width), BF16),
            jax.ShapeDtypeStruct((width, quarter), BF16),
            jax.ShapeDtypeStruct((width, quarter), BF16),
        ),
        in_specs=[vmem] + [hbm] * 3,
        out_specs=(hbm, hbm, hbm),
        scratch_shapes=[
            pltpu.VMEM((CHUNKS, n_e, SLAB, oct_w), BF16),
            pltpu.VMEM((CHUNKS * n_e * PER, width), BF16),
            pltpu.VMEM((OCT, toks, oct_w), BF16),
            pltpu.VMEM((2, width, quarter), BF16),
            dma((CHUNKS,)),
            dma((OCT,)),
            dma((OCT,)),
            dma((OCT,)),
        ],
        compiler_params=pltpu.CompilerParams(vmem_limit_bytes=60 * 2**20),
    )(ids_row, back, gate_grad, up_grad)
    return token_grad, gate_grad[None], up_grad[None]


def solution(mesh):
    in_specs = (
        P(("dp", "expert"), None),
        P(("dp", "expert"), None),
        P(("dp", "expert"), None),
        P(("dp", "expert"), None),
        P("expert", None, "dp"),
        P("expert", None, "dp"),
        P("expert", "dp", None),
    )
    out_specs = (P(("dp", "expert"), None), P("expert", None, "dp"), P("expert", None, "dp"))
    return jax.shard_map(local, mesh=mesh, in_specs=in_specs, out_specs=out_specs, check_vma=False)
```
